128 devices in a mesh: comp: 4 (over y_hi, core), pts: 32 (over x, z, y_lo).
Axes of the slice: x: 4, y: 4 (y_hi: 2, y_lo: 2; y = y_hi * 2 + y_lo), z: 4, core: 2. Of those that a mesh axis runs over, the one named last changes fastest.
Arguments:
- spectra: float32 [1800, 256, 256], P('comp', 'pts'), may hold values from 0 to 18, as said below
- land_mask: int32 [256, 256], P('pts'), may hold values 0 or 1
- courant: float32 [50], replicated, may hold values from 0.05 to 0.6
- wind_speed: float32 [256, 256], P('pts'), may hold values from 0.5 to 2
- wind_angle: float32 [256, 256], P('pts'), may hold values from -3.140625 to 3.140625
- growth: float32 [50], replicated, may hold values from 0.1 to 0.5
- whitecap: float32 [50], replicated, may hold values from 0.1 to 0.5
- coupling: bfloat16 [1800, 1800], replicated, may hold values from -0.125 to 0.125
Outputs:
- updated_spectra: float32 [1800, 256, 256], P('comp', 'pts')
The draws below stay inside these ranges and needn't reach their ends.
Inputs may be any that keep to these rules, and one draw needn't show every extreme that they name: `spectra`: positive spectral densities.
All inputs are finite; a program needn't handle non-finite values. No bound on the sum of `land_mask` on one device may be relied on, other than what follows from the above.
Results may differ from the reference program's by a relative error of at most 0.0018.
Values sent between devices are 32-bit elements; how exact they have to be, the bound alone decides.
No kernel may reach another device: no remote copies, remote signals or barrier semaphores. Data moves between devices by JAX's collectives and lax.ppermute only.
A program may use at most 128 MiB of HBM per device.

```python
import math
import jax
import jax.numpy as jnp
from jax import lax

NF = 50
ND = 36
NXG = 256
SUBSTEPS = 3
NC = 1800
NY = 256


def draw_spectra(key, part):
    key = jax.random.fold_in(key, 17)
    point_key, freq_key, rough_key = jax.random.split(key, 3)
    point_scale = jnp.exp(jax.random.uniform(point_key, (NY, NXG), jnp.float32, math.log(0.3), math.log(3.0)))
    freq_scale = jnp.exp(jax.random.uniform(freq_key, (NF,), jnp.float32, math.log(0.3), math.log(3.0)))
    roughness = jax.random.uniform(rough_key, (NF, ND, NY, NXG), jnp.float32, 0.4, 1.6)
    values = freq_scale[:, None, None, None] * point_scale[None, None] * roughness
    return values.reshape(NF * ND, NY, NXG)


def plant(entries, rng, least, high):
    longest = entries.shape.index(max(entries.shape))
    spots = []
    for shift in (0, 1):
        where = [jax.random.randint(jax.random.fold_in(rng, axis), (), 0, length) for axis, length in enumerate(entries.shape)]
        where[longest] = (where[longest] + shift) % entries.shape[longest]
        spots.append(tuple(where))
    return entries.at[spots[0]].set(least).at[spots[1]].set(high)


def levels(own_key, shape, cuts, low, largest):
    gain = 1.0
    for dim, parts in cuts:
        steps = jax.random.uniform(jax.random.fold_in(jax.random.fold_in(own_key, 6), dim), (parts,), jnp.float32, low / len(cuts), largest / len(cuts))
        gain = gain * jnp.repeat(jnp.exp(steps), shape[dim] // parts).reshape((-1,) + (1,) * (len(shape) - 1 - dim))
    return gain


def gaussian(key, shape, width, reach, kind=jnp.bfloat16):
    result = width * jax.random.normal(key, shape, jnp.float32)
    return jnp.clip(result, min=-reach, max=reach).astype(kind)


def setup_inputs(seed: int = 0) -> dict:
    keys = jax.random.split(jax.random.key(seed), 9)
    return {
        "spectra": draw_spectra(jax.random.fold_in(keys[8], 71), 0),
        "land_mask": plant((jax.random.randint(keys[1], (NY, NXG), 0, 4) < 3).astype(jnp.int32), jax.random.fold_in(keys[1], 1), 0, 1),
        "courant": jnp.clip(jnp.exp(jax.random.uniform(keys[2], (NF,), jnp.float32, math.log(0.05), math.log(0.6))), 0.05, 0.6),
        "wind_speed": jnp.clip(jnp.exp(math.log(2.0) - 1.3862944 * jax.random.uniform(keys[3], (NY, NXG), jnp.float32) ** levels(keys[3], (NY, NXG), ((0, 32),), -0.2, 0.2)), 0.5, 2.0),
        "wind_angle": jnp.clip(jax.random.uniform(keys[4], (NY, NXG), jnp.float32, -3.140625, 3.140625), -3.140625, 3.140625),
        "growth": jnp.clip(jnp.exp(jax.random.uniform(keys[5], (NF,), jnp.float32, math.log(0.1), math.log(0.5))), 0.1, 0.5),
        "whitecap": jnp.clip(jnp.exp(jax.random.uniform(keys[6], (NF,), jnp.float32, math.log(0.1), math.log(0.5))), 0.1, 0.5),
        "coupling": gaussian(keys[7], (NC, NC), NC ** -0.5, 0.125),
    }


substep = 0.5


def upwind_step(spectrum, sea_mask, speed_east, speed_north, south_side, north_side):
    padded_x = jnp.pad(spectrum, ((0, 0), (0, 0), (1, 1)))
    west_side = padded_x[:, :, :-2]
    east_side = padded_x[:, :, 2:]
    east_going = jnp.maximum(speed_east, 0.0)[:, None, None]
    west_going = jnp.minimum(speed_east, 0.0)[:, None, None]
    north_going = jnp.maximum(speed_north, 0.0)[:, None, None]
    south_going = jnp.minimum(speed_north, 0.0)[:, None, None]
    updated = spectrum - east_going * (spectrum - west_side) - west_going * (east_side - spectrum) - north_going * (spectrum - south_side) - south_going * (north_side - spectrum)
    return updated * sea_mask


def source_terms(spectrum, celerity, heading, growth_rate, whitecap_rate, bearing_all, coupling):
    facing = 0.5 * (1.0 + jnp.cos(bearing_all[:, None] - heading[None, :]))
    input_rate = growth_rate[:, None] * celerity[None, :] * (facing * facing)
    for repeat in range(SUBSTEPS):
        rounded = spectrum.astype(jnp.bfloat16)
        transfer = jnp.dot(coupling, rounded, preferred_element_type=jnp.float32)
        mean_square = jnp.mean(spectrum * spectrum, axis=0)
        damping = mean_square / (1.0 + mean_square)
        net_rate = input_rate - whitecap_rate[:, None] * damping[None, :]
        spectrum = spectrum + substep * (transfer + net_rate * spectrum)
    return spectrum


def reference(spectra, land_mask, courant, wind_speed, wind_angle, growth, whitecap, coupling):
    sea_mask = land_mask.astype(jnp.float32)
    bearing = (jnp.arange(ND, dtype=jnp.float32) + 0.5) * (2.0 * math.pi / ND)
    cosine = jnp.cos(bearing)
    sine_part = jnp.sin(bearing)
    blocks = spectra.reshape(NF, ND, NY, NXG)

    def advect(inputs):
        spectrum, celerity = inputs
        spectrum = spectrum * sea_mask
        padded_y = jnp.pad(spectrum, ((0, 0), (1, 1), (0, 0)))
        return upwind_step(spectrum, sea_mask, celerity * cosine, celerity * sine_part, padded_y[:, :-2], padded_y[:, 2:])

    advected = lax.map(advect, (blocks, courant))
    by_rows = jnp.moveaxis(advected, 2, 0)
    growth_rate = jnp.repeat(growth, ND)
    whitecap_rate = jnp.repeat(whitecap, ND)
    bearing_all = jnp.tile(bearing, NF)

    def one_row(inputs):
        spectrum, celerity, heading = inputs
        return source_terms(spectrum.reshape(NC, NXG), celerity, heading, growth_rate, whitecap_rate, bearing_all, coupling)

    finished = lax.map(one_row, (by_rows, wind_speed, wind_angle))
    return jnp.moveaxis(finished, 0, 1)
```

```python
import functools
import math

import jax
import jax.numpy as jnp
from jax import lax
from jax.experimental import pallas as pl
from jax.experimental.pallas import tpu as pltpu
from jax.sharding import PartitionSpec as P
import numpy as np

NF = 50
ND = 36
HALF = ND // 2
SUBSTEPS = 3
substep = 0.5

GROUP = 450
SENT = 456
HELD = 464
GROUPS = 4
ALL = GROUPS * GROUP
BLOCKS = GROUP // HALF
PACKED = (BLOCKS + 1) // 2 * HALF
ROWS = 8
COLS = 256
LANES = 128
LINES = ROWS * COLS // LANES
ORDER = (1, 2, 3, 4, 5, 6, 0, 7)
INNER = 6 * COLS
POINTS = ROWS * COLS
SLOTS = 256
CHUNK = 2 * SLOTS
EARLY = 1
CHUNKS = POINTS // CHUNK
TILE = 16
CUTS = (0, 464, 928, 1392, ALL)
LOWER = 896
MIB = 1 << 20
f32 = jnp.float32
bf16 = jnp.bfloat16

WHOLE = pl.BlockSpec(memory_space=pltpu.VMEM)
SCALAR = pl.BlockSpec(memory_space=pltpu.SMEM)
UNREAD = pl.BlockSpec(memory_space=pl.ANY)


def grid_row(ref, first, count, y):
    halves = [ref[pl.ds(first * LINES + h * ROWS + y, count, stride=LINES), :] for h in range(COLS // LANES)]
    return jnp.concatenate(halves, axis=1)


def split(values):
    high = values.astype(bf16)
    return high, (values - high.astype(f32)).astype(bf16)


def in_order(values):
    return jnp.concatenate([values[y : y + 1] for y in ORDER], axis=0)


def numbered(first, count):
    k = (lax.broadcasted_iota(jnp.int32, (count, LANES), 0) + first).astype(f32)
    frequency = jnp.floor((k + 0.5) * (1.0 / ND))
    return frequency, k - ND * frequency


def look_up(index, table):
    lane = lax.broadcasted_iota(jnp.int32, index.shape, 1).astype(f32)
    return jnp.sum(jnp.where(index == lane, table, 0.0), axis=1, keepdims=True)


def columns(values, count):
    lane = lax.broadcasted_iota(jnp.int32, (count, LANES), 1)
    return sum(jnp.where(lane == i, column, 0.0) for i, column in enumerate(values))


def pack_kernel(place_ref, spec_ref, land_ref, up_ref, down_ref):
    core = place_ref[1]
    south_row = land_ref[0:1, :].astype(f32)
    north_row = land_ref[ROWS - 1 : ROWS, :].astype(f32)

    def pack(parity):
        for b in range((BLOCKS + 1) // 2):
            north_going = min(2 * b + parity, BLOCKS - 1) * HALF
            south_going = min(2 * b + 1 - parity, BLOCKS - 1) * HALF
            at = slice(b * HALF, (b + 1) * HALF)
            up_ref[at, :] = grid_row(spec_ref, north_going, HALF, ROWS - 1) * north_row
            down_ref[at, :] = grid_row(spec_ref, south_going, HALF, 0) * south_row

    for parity in (0, 1):
        pl.when(core == parity)(functools.partial(pack, parity))


def slot_rows(core, first, shape):
    number = lax.broadcasted_iota(jnp.int32, shape, 0)
    return (first + jnp.where(number < SLOTS, number + core * SLOTS, number - core * SLOTS)).astype(f32)


def place_points(slots_ref, pick_ref, core, first, lanes):
    number = slot_rows(core, first, (CHUNK, COLS))
    for i in range(lanes // COLS):
        hit = slots_ref[i : i + 1, :] == number
        pick_ref[:, i * COLS : (i + 1) * COLS] = jnp.where(hit, 1.0, 0.0).astype(bf16)


def contract(a, b):
    return lax.dot_general(a, b, (((1,), (1,)), ((), ())), preferred_element_type=f32)


def advect_kernel(
    place_ref, spec_ref, land_ref, courant_ref, ways_ref, wind_ref, angle_ref, after_ref,
    slots_ref, speed_ref, high_ref, low_ref, edge_ref, *rest,
):
    sent, (sea_ref, pick_ref, tail_ref) = rest[:-3], rest[-3:]
    group, core = place_ref[0], place_ref[1]
    sea = in_order(land_ref[...]).astype(f32)
    sea_ref[...] = sea

    ramp = [lax.broadcasted_iota(jnp.int32, (COLS, COLS), axis) for axis in (0, 1)]
    upper = jnp.where(ramp[0] <= ramp[1], 1.0, 0.0).astype(bf16)
    running = jnp.dot(sea.astype(bf16), upper, preferred_element_type=f32)
    before = jnp.zeros((1, 1), f32)
    for i in range(ROWS):
        if i == 6:
            before = jnp.maximum(before, EARLY * CHUNK * 1.0)
        slots_ref[i : i + 1, :] = jnp.where(
            sea[i : i + 1] > 0.0, running[i : i + 1] - 1.0 + before, -1.0
        )
        before = before + running[i : i + 1, COLS - 1 :]

    frequency, direction = numbered(group * GROUP, HELD)
    speed = look_up(frequency, courant_ref[...])
    speed_ref[...] = columns([speed * look_up(direction, ways_ref[i : i + 1, :]) for i in range(4)], HELD)

    lane = lax.broadcasted_iota(jnp.int32, (1, COLS), 1)
    not_first = jnp.where(lane > 0, 1.0, 0.0)
    not_last = jnp.where(lane < COLS - 1, 1.0, 0.0)

    def advect(first, count, store):
        speeds = [
            jnp.broadcast_to(speed_ref[pl.ds(first, count), i : i + 1], (count, COLS)) for i in range(4)
        ]
        east_going, west_going, north_going, south_going = speeds

        def row(y):
            i = ORDER.index(y)
            return grid_row(spec_ref, first, count, y) * sea_ref[i : i + 1, :]

        before, here = None, row(0)
        for y in range(ROWS):
            after = row(y + 1) if y < ROWS - 1 else None
            west = pltpu.roll(here, 1, 1) * not_first
            east = pltpu.roll(here, COLS - 1, 1) * not_last
            moved = here - east_going * (here - west) - west_going * (east - here)
            moved = moved - north_going * (here - before if before is not None else here)
            moved = moved - south_going * (after - here if after is not None else -here)
            i = ORDER.index(y)
            store(i, moved * sea_ref[i : i + 1, :])
            before, here = here, after

    def keep(first):
        def store(i, values):
            if i < 6:
                at = slice(i * COLS, (i + 1) * COLS)
                high, low = split(values)
                high_ref[pl.ds(first, TILE), at] = high
                low_ref[pl.ds(first, TILE), at] = low
            else:
                edge_ref[i - 6, pl.ds(first, TILE), :] = values

        return store

    def step(t, carry):
        first = pl.multiple_of(t * TILE, TILE)
        advect(first, TILE, keep(first))
        return carry

    full = GROUP // TILE
    lax.fori_loop(0, full, step, 0)
    last = full * TILE
    left = GROUP - last
    tail_ref[...] = jnp.zeros_like(tail_ref)

    def keep_tail(i, values):
        tail_ref[i, 0:left, :] = values

    advect(last, left, keep_tail)
    angle = in_order(angle_ref[...])
    for j, values in enumerate((in_order(wind_ref[...]), jnp.cos(angle), jnp.sin(angle))):
        for i in range(ROWS):
            tail_ref[i, left + j : left + j + 1, :] = values[i : i + 1]
    for i in range(ROWS):
        if i < 6:
            at = slice(i * COLS, (i + 1) * COLS)
            high, low = split(tail_ref[i])
            high_ref[last : last + TILE, at] = high
            low_ref[last : last + TILE, at] = low
        else:
            edge_ref[i - 6, last : last + TILE, :] = tail_ref[i]

    for m in range(EARLY):
        place_points(slots_ref, pick_ref, core, m * CHUNK, INNER)
        chosen = contract(high_ref[...], pick_ref[...]) + contract(low_ref[...], pick_ref[...])
        sent[2 * m][...] = chosen[:SENT, :SLOTS]
        sent[2 * m + 1][...] = chosen[:SENT, SLOTS:]


def rest_kernel(
    chunks, place_ref, high_ref, low_ref, edge_ref, south_ref, north_ref, land_ref, slots_ref, speed_ref, *rest
):
    sent, (pick_ref, fixed_ref, edge_high, edge_low) = rest[:-4], rest[-4:]
    core = place_ref[1]
    fixed_ref[...] = edge_ref[...]
    south_row = land_ref[0:1, :].astype(f32)
    north_row = land_ref[ROWS - 1 : ROWS, :].astype(f32)

    def fix(parity):
        for b in range((BLOCKS + 1) // 2):
            at = slice(b * HALF, (b + 1) * HALF)
            north_going, south_going = 2 * b + parity, 2 * b + 1 - parity
            if north_going < BLOCKS:
                mine = slice(north_going * HALF, (north_going + 1) * HALF)
                speed = jnp.broadcast_to(speed_ref[mine, 2:3], (HALF, COLS))
                fixed_ref[0, mine, :] += speed * south_ref[at, :] * south_row
            if south_going < BLOCKS:
                mine = slice(south_going * HALF, (south_going + 1) * HALF)
                speed = jnp.broadcast_to(speed_ref[mine, 3:4], (HALF, COLS))
                fixed_ref[1, mine, :] -= speed * north_ref[at, :] * north_row

    for parity in (0, 1):
        pl.when(core == parity)(functools.partial(fix, parity))
    for i in range(2):
        at = slice(i * COLS, (i + 1) * COLS)
        edge_high[:, at], edge_low[:, at] = split(fixed_ref[i])

    for m in range(EARLY, chunks):
        place_points(slots_ref, pick_ref, core, m * CHUNK, POINTS)
        inner, edge = pick_ref[:, :INNER], pick_ref[:, INNER:]
        chosen = (
            contract(high_ref[...], inner)
            + contract(low_ref[...], inner)
            + contract(edge_high[...], edge)
            + contract(edge_low[...], edge)
        )
        sent[2 * (m - EARLY)][...] = chosen[:SENT, :SLOTS]
        sent[2 * (m - EARLY) + 1][...] = chosen[:SENT, SLOTS:]


def rates_kernel(ways_ref, growth_ref, whitecap_ref, rate_ref):
    frequency, direction = numbered(0, ALL)
    rate_ref[...] = columns(
        [
            look_up(direction, ways_ref[4:5, :]),
            look_up(direction, ways_ref[5:6, :]),
            substep * look_up(frequency, growth_ref[...]),
            substep * look_up(frequency, whitecap_ref[...]),
        ],
        ALL,
    )


def source_kernel(
    place_ref, own_ref, pair_ref, far_ref, cross_ref, coupling_ref, rate_ref, out_ref, back_ref,
    state_ref, rounded_ref, input_ref,
):
    group = place_ref[0]

    def load(g):
        for q, ref in enumerate((own_ref, pair_ref, far_ref, cross_ref)):
            first = (g ^ q) * GROUP
            state_ref[first : first + GROUP, :] = ref[:GROUP, :]

    for g in range(GROUPS):
        pl.when(group == g)(functools.partial(load, g))
    speed, cosine, sine = (own_ref[GROUP + j : GROUP + j + 1, :] for j in range(3))

    total = jnp.zeros((1, SLOTS), f32)
    for start, stop in zip(CUTS[:-1], CUTS[1:]):
        at = slice(start, stop)
        column = lambda i: jnp.broadcast_to(rate_ref[at, i : i + 1], (stop - start, SLOTS))
        facing = 0.5 + 0.5 * (column(0) * cosine + column(1) * sine)
        input_ref[at, :] = column(2) * speed * (facing * facing)
        state = state_ref[at, :]
        rounded_ref[0, at, :] = state.astype(bf16)
        total = total + jnp.sum(state * state, axis=0, keepdims=True)

    def update(at, step, damping, count):
        transfer = jnp.dot(coupling_ref[at, :], rounded_ref[step % 2], preferred_element_type=f32)
        state = state_ref[at, :]
        whitecap = jnp.broadcast_to(rate_ref[at, 3:4], (count, SLOTS))
        return state + (substep * transfer + (input_ref[at, :] - whitecap * damping) * state)

    for step in range(SUBSTEPS):
        mean_square = total * (1.0 / ALL)
        damping = mean_square / (1.0 + mean_square)
        total = jnp.zeros((1, SLOTS), f32)
        if step < SUBSTEPS - 1:
            for start, stop in zip(CUTS[:-1], CUTS[1:]):
                at = slice(start, stop)
                values = update(at, step, damping, stop - start)
                state_ref[at, :] = values
                rounded_ref[(step + 1) % 2, at, :] = values.astype(bf16)
                total = total + jnp.sum(values * values, axis=0, keepdims=True)
        else:
            here = (group // 2) * LOWER
            for start, count in ((0, 464), (464, ALL - LOWER - 464)):
                at = pl.ds(pl.multiple_of(here + start, TILE), count)
                state_ref[at, :] = update(at, step, damping, count)

    def give(g):
        out_ref[:GROUP, :] = state_ref[g * GROUP : (g + 1) * GROUP, :]
        back_ref[:GROUP, :] = state_ref[(g ^ 1) * GROUP : ((g ^ 1) + 1) * GROUP, :]

    for g in range(GROUPS):
        pl.when(group == g)(functools.partial(give, g))


def spread(place_ref, slots_ref, pick_ref, first_chunk, own, came, add):
    core = place_ref[1]
    for n in range(len(own)):
        place_points(slots_ref, pick_ref, core, (first_chunk + n) * CHUNK, POINTS)
        values = jnp.concatenate([own[n][...], came[n][...]], axis=1)
        high, low = split(values)
        for i in range(ROWS):
            at = slice(i * COLS, (i + 1) * COLS)
            add(
                n,
                i,
                jnp.dot(high, pick_ref[:, at], preferred_element_type=f32)
                + jnp.dot(low, pick_ref[:, at], preferred_element_type=f32),
            )


def gather_kernel(first_chunk, count, place_ref, slots_ref, *rest):
    own, came, (sum_ref, pick_ref) = rest[:count], rest[count : 2 * count], rest[2 * count :]

    def add(n, i, values):
        at = slice(i * COLS, (i + 1) * COLS)
        if n:
            sum_ref[:, at] += values
        else:
            sum_ref[:, at] = values

    spread(place_ref, slots_ref, pick_ref, first_chunk, own, came, add)


def finish_kernel(first_chunk, place_ref, slots_ref, sum_ref, own_ref, came_ref, out_ref, pick_ref):
    def add(n, i, values):
        at = slice(i * COLS, (i + 1) * COLS)
        values = values[:GROUP] + sum_ref[:GROUP, at]
        for h in range(COLS // LANES):
            lines = pl.ds(h * ROWS + ORDER[i], GROUP, stride=LINES)
            out_ref[lines, :] = values[:, h * LANES : (h + 1) * LANES]

    spread(place_ref, slots_ref, pick_ref, first_chunk, (own_ref,), (came_ref,), add)


def call(kernel, out, flops, scratch=(), scalars=1, inputs=0, unread=0, mib=32, moved=8 * MIB):
    return pl.pallas_call(
        kernel,
        out_shape=out,
        in_specs=[SCALAR] * scalars + [WHOLE] * inputs + [UNREAD] * unread,
        out_specs=jax.tree.map(lambda _: WHOLE, out),
        scratch_shapes=list(scratch),
        compiler_params=pltpu.CompilerParams(vmem_limit_bytes=mib * MIB),
        cost_estimate=pl.CostEstimate(flops=flops, bytes_accessed=moved, transcendentals=0),
    )


def pairs(flip):
    return [(g, g ^ flip) for g in range(GROUPS)]


def ways():
    bearing = (np.arange(ND) + 0.5) * (2.0 * math.pi / ND)
    cosine, sine = np.cos(bearing), np.sin(bearing)
    rows = [np.maximum(cosine, 0), np.minimum(cosine, 0), np.maximum(sine, 0), np.minimum(sine, 0), cosine, sine]
    table = np.zeros((ROWS, LANES), np.float32)
    table[: len(rows), :ND] = rows
    return jnp.asarray(table)


def by_lane(values):
    return jnp.pad(values, (0, LANES - NF))[None, :]


def on_device(spectra, land_mask, courant, wind_speed, wind_angle, growth, whitecap, coupling):
    group = lax.axis_index("comp")
    place = jnp.stack([group, group % 2]).astype(jnp.int32)
    spec = spectra.reshape(GROUP, ROWS, COLS // LANES, LANES).swapaxes(1, 2).reshape(GROUP * LINES, LANES)

    halo = jax.ShapeDtypeStruct((PACKED, COLS), f32)
    up, down = call(pack_kernel, (halo, halo), 10**6, inputs=2)(place, spec, land_mask)
    count = lax.axis_size("pts")
    south = lax.ppermute(up, "pts", [(i, i + 1) for i in range(count - 1)])
    north = lax.ppermute(down, "pts", [(i + 1, i) for i in range(count - 1)])

    message = jax.ShapeDtypeStruct((SENT, SLOTS), f32)
    inner = jax.ShapeDtypeStruct((HELD, INNER), bf16)
    slots, speeds, high, low, edge, *early = call(
        advect_kernel,
        (
            jax.ShapeDtypeStruct((ROWS, COLS), f32),
            jax.ShapeDtypeStruct((HELD, LANES), f32),
            inner,
            inner,
            jax.ShapeDtypeStruct((2, HELD, COLS), f32),
        )
        + (message,) * (2 * EARLY),
        2 * 10**9,
        [pltpu.VMEM((ROWS, COLS), f32), pltpu.VMEM((CHUNK, INNER), bf16), pltpu.VMEM((ROWS, TILE, COLS), f32)],
        inputs=6,
        unread=1,
    )(place, spec, land_mask, by_lane(courant), ways(), wind_speed, wind_angle, up)

    late = call(
        functools.partial(rest_kernel, CHUNKS),
        (message,) * (2 * (CHUNKS - EARLY)),
        6 * 10**9,
        [
            pltpu.VMEM((CHUNK, POINTS), bf16),
            pltpu.VMEM((2, HELD, COLS), f32),
            pltpu.VMEM((HELD, POINTS - INNER), bf16),
            pltpu.VMEM((HELD, POINTS - INNER), bf16),
        ],
        inputs=8,
    )(place, high, low, edge, south, north, land_mask, slots, speeds)
    messages = list(early) + list(late)
    own, other = messages[0::2], messages[1::2]

    rates = call(rates_kernel, jax.ShapeDtypeStruct((ALL, LANES), f32), 10**6, scalars=0, inputs=3)(
        ways(), by_lane(growth), by_lane(whitecap)
    )

    outs, came = [], []
    for m in range(CHUNKS):
        far = lax.ppermute(own[m], "comp", pairs(2))
        cross = lax.ppermute(other[m], "comp", pairs(3))
        pair = lax.ppermute(other[m], "comp", pairs(1))
        out, back = call(
            source_kernel,
            (message, message),
            4 * 10**9,
            [pltpu.VMEM((ALL, SLOTS), f32), pltpu.VMEM((2, ALL, SLOTS), bf16), pltpu.VMEM((ALL, SLOTS), f32)],
            inputs=6,
        )(place, own[m], pair, far, cross, coupling, rates)
        outs.append(out)
        came.append(lax.ppermute(back, "comp", pairs(1)))

    first = CHUNKS - 1
    total = call(
        functools.partial(gather_kernel, 0, first),
        jax.ShapeDtypeStruct((SENT, POINTS), f32),
        7 * 10**9,
        [pltpu.VMEM((CHUNK, POINTS), bf16)],
        inputs=1 + 2 * first,
    )(place, slots, *outs[:first], *came[:first])
    finished = call(
        functools.partial(finish_kernel, first),
        jax.ShapeDtypeStruct((GROUP * LINES, LANES), f32),
        2 * 10**9,
        [pltpu.VMEM((CHUNK, POINTS), bf16)],
        inputs=4,
    )(place, slots, total, outs[first], came[first])
    return finished.reshape(GROUP, COLS // LANES, ROWS, LANES).swapaxes(1, 2).reshape(GROUP, ROWS, COLS)


def solution(mesh):
    placed = (
        P("comp", "pts", None),
        P("pts", None),
        P(),
        P("pts", None),
        P("pts", None),
        P(),
        P(),
        P(),
    )
    return jax.shard_map(
        on_device, mesh=mesh, in_specs=placed, out_specs=P("comp", "pts", None), check_vma=False
    )
```

```python
import functools
import math

import jax
import jax.numpy as jnp
from jax import lax
from jax.experimental import pallas as pl
from jax.experimental.pallas import tpu as pltpu
from jax.sharding import PartitionSpec as P
import numpy as np

NF = 50
ND = 36
HALF = ND // 2
SUBSTEPS = 3
substep = 0.5

GROUP = 450
SENT = 456
HELD = 480
GROUPS = 4
ALL = GROUPS * GROUP
BLOCKS = GROUP // HALF
PACKED = (BLOCKS + 1) // 2 * HALF
ROWS = 8
COLS = 256
LANES = 128
LINES = ROWS * COLS // LANES
ORDER = (1, 2, 3, 4, 5, 6, 0, 7)
INNER = 6 * COLS
POINTS = ROWS * COLS
SLOTS = 256
CHUNK = 2 * SLOTS
BESIDE = 3
FOLD = 2 * BESIDE
FEW = LANES // BESIDE
FOLDED = HELD // FOLD
MOST = SLOTS + FEW
WIDE = SLOTS + LANES
FIRST = 2 * MOST
CHUNKS = 2
USUAL = FIRST + CHUNKS * CHUNK
SENT_FIRST = SENT + FOLDED
TILE = 16
CUTS = (0, 464, 928, 1392, ALL)
LOWER = 896
MIB = 1 << 20
f32 = jnp.float32
bf16 = jnp.bfloat16

WHOLE = pl.BlockSpec(memory_space=pltpu.VMEM)
SCALAR = pl.BlockSpec(memory_space=pltpu.SMEM)
UNREAD = pl.BlockSpec(memory_space=pl.ANY)


def grid_row(ref, first, count, y):
    halves = [ref[pl.ds(first * LINES + h * ROWS + y, count, stride=LINES), :] for h in range(COLS // LANES)]
    return jnp.concatenate(halves, axis=1)


def split(values):
    high = values.astype(bf16)
    return high, (values - high.astype(f32)).astype(bf16)


def in_order(values):
    return jnp.concatenate([values[y : y + 1] for y in ORDER], axis=0)


def numbered(first, count):
    k = (lax.broadcasted_iota(jnp.int32, (count, LANES), 0) + first).astype(f32)
    frequency = jnp.floor((k + 0.5) * (1.0 / ND))
    return frequency, k - ND * frequency


def look_up(index, table):
    lane = lax.broadcasted_iota(jnp.int32, index.shape, 1).astype(f32)
    return jnp.sum(jnp.where(index == lane, table, 0.0), axis=1, keepdims=True)


def columns(values, count):
    lane = lax.broadcasted_iota(jnp.int32, (count, LANES), 1)
    return sum(jnp.where(lane == i, column, 0.0) for i, column in enumerate(values))


def pack_kernel(place_ref, spec_ref, land_ref, up_ref, down_ref):
    core = place_ref[1]
    south_row = land_ref[0:1, :].astype(f32)
    north_row = land_ref[ROWS - 1 : ROWS, :].astype(f32)

    def pack(parity):
        for b in range((BLOCKS + 1) // 2):
            north_going = min(2 * b + parity, BLOCKS - 1) * HALF
            south_going = min(2 * b + 1 - parity, BLOCKS - 1) * HALF
            at = slice(b * HALF, (b + 1) * HALF)
            up_ref[at, :] = grid_row(spec_ref, north_going, HALF, ROWS - 1) * north_row
            down_ref[at, :] = grid_row(spec_ref, south_going, HALF, 0) * south_row

    for parity in (0, 1):
        pl.when(core == parity)(functools.partial(pack, parity))


def match(slots_ref, pick_ref, number, lanes):
    number = number.astype(f32)
    for i in range(lanes // COLS):
        hit = slots_ref[i : i + 1, :] == number
        pick_ref[: number.shape[0], i * COLS : (i + 1) * COLS] = jnp.where(hit, 1.0, 0.0).astype(bf16)


def lines(count):
    line = lax.broadcasted_iota(jnp.int32, (2 * count, COLS), 0)
    side = jnp.where(line < count, 0, 1)
    return side, line - count * side


def slots_of(core, chunk):
    side, place = lines(WIDE if chunk is None else SLOTS)
    side = jnp.bitwise_xor(core, side)
    if chunk is None:
        return jnp.where(place < MOST, side * MOST + place, -2)
    return FIRST + chunk * CHUNK + side * SLOTS + place


def contract(a, b):
    return lax.dot_general(a, b, (((1,), (1,)), ((), ())), preferred_element_type=f32)


def advect_kernel(
    place_ref, spec_ref, land_ref, courant_ref, ways_ref, wind_ref, angle_ref, after_ref,
    used_ref, slots_ref, speed_ref, high_ref, low_ref, edge_ref, *rest,
):
    sent, (sea_ref, pick_ref, tail_ref) = rest[:-3], rest[-3:]
    group, core = place_ref[0], place_ref[1]
    sea = in_order(land_ref[...]).astype(f32)
    sea_ref[...] = sea

    ramp = [lax.broadcasted_iota(jnp.int32, (COLS, COLS), axis) for axis in (0, 1)]
    upper = jnp.where(ramp[0] <= ramp[1], 1.0, 0.0).astype(bf16)
    running = jnp.dot(sea.astype(bf16), upper, preferred_element_type=f32)
    before = jnp.zeros((1, 1), f32)
    for i in range(ROWS):
        if i == 6:
            before = jnp.maximum(before, 1.0 * FIRST)
        slots_ref[i : i + 1, :] = jnp.where(
            sea[i : i + 1] > 0.0, running[i : i + 1] - 1.0 + before, -1.0
        )
        before = before + running[i : i + 1, COLS - 1 :]
    used_ref[0] = jnp.max(before).astype(jnp.int32)

    frequency, direction = numbered(group * GROUP, HELD)
    speed = look_up(frequency, courant_ref[...])
    speed_ref[...] = columns([speed * look_up(direction, ways_ref[i : i + 1, :]) for i in range(4)], HELD)

    lane = lax.broadcasted_iota(jnp.int32, (1, COLS), 1)
    not_first = jnp.where(lane > 0, 1.0, 0.0)
    not_last = jnp.where(lane < COLS - 1, 1.0, 0.0)

    def advect(first, count, store):
        speeds = [
            jnp.broadcast_to(speed_ref[pl.ds(first, count), i : i + 1], (count, COLS)) for i in range(4)
        ]
        east_going, west_going, north_going, south_going = speeds

        def row(y):
            i = ORDER.index(y)
            return grid_row(spec_ref, first, count, y) * sea_ref[i : i + 1, :]

        before, here = None, row(0)
        for y in range(ROWS):
            after = row(y + 1) if y < ROWS - 1 else None
            west = pltpu.roll(here, 1, 1) * not_first
            east = pltpu.roll(here, COLS - 1, 1) * not_last
            moved = here - east_going * (here - west) - west_going * (east - here)
            moved = moved - north_going * (here - before if before is not None else here)
            moved = moved - south_going * (after - here if after is not None else -here)
            i = ORDER.index(y)
            store(i, moved * sea_ref[i : i + 1, :])
            before, here = here, after

    def keep(first):
        def store(i, values):
            if i < 6:
                at = slice(i * COLS, (i + 1) * COLS)
                high, low = split(values)
                high_ref[pl.ds(first, TILE), at] = high
                low_ref[pl.ds(first, TILE), at] = low
            else:
                edge_ref[i - 6, pl.ds(first, TILE), :] = values

        return store

    def step(t, carry):
        first = pl.multiple_of(t * TILE, TILE)
        advect(first, TILE, keep(first))
        return carry

    full = GROUP // TILE
    lax.fori_loop(0, full, step, 0)
    last = full * TILE
    left = GROUP - last
    tail_ref[...] = jnp.zeros_like(tail_ref)
    rest_of = slice(last + TILE, HELD)
    for ref in (high_ref, low_ref):
        ref[rest_of, :] = jnp.zeros((HELD - last - TILE, INNER), bf16)
    edge_ref[:, rest_of, :] = jnp.zeros((2, HELD - last - TILE, COLS), f32)

    def keep_tail(i, values):
        tail_ref[i, 0:left, :] = values

    advect(last, left, keep_tail)
    angle = in_order(angle_ref[...])
    for j, values in enumerate((in_order(wind_ref[...]), jnp.cos(angle), jnp.sin(angle))):
        for i in range(ROWS):
            tail_ref[i, left + j : left + j + 1, :] = values[i : i + 1]
    for i in range(ROWS):
        if i < 6:
            at = slice(i * COLS, (i + 1) * COLS)
            high, low = split(tail_ref[i])
            high_ref[last : last + TILE, at] = high
            low_ref[last : last + TILE, at] = low
        else:
            edge_ref[i - 6, last : last + TILE, :] = tail_ref[i]

    def picked(number):
        match(slots_ref, pick_ref, number, INNER)
        pick = pick_ref[: number.shape[0], :]
        return contract(high_ref[...], pick) + contract(low_ref[...], pick)

    side, place = lines(LANES)
    number = jnp.bitwise_xor(core, side) * MOST + SLOTS + place
    few = picked(jnp.where(place < FEW, number, -2))
    for i, ref in enumerate(sent):
        for half in range(FOLD // BESIDE):
            runs = [few[(half * BESIDE + r) * FOLDED :][:FOLDED, i * LANES : (i + 1) * LANES] for r in range(BESIDE)]
            runs = [pltpu.roll(values, r * FEW, 1) if r else values for r, values in enumerate(runs)]
            ref[SENT:, half * LANES : (half + 1) * LANES] = sum(runs)
    side, place = lines(SLOTS)
    chosen = picked(jnp.bitwise_xor(core, side) * MOST + place)
    for i, ref in enumerate(sent):
        ref[:SENT, :] = chosen[:SENT, i * SLOTS : (i + 1) * SLOTS]


def choose(place_ref, slots_ref, pick_ref, chunk, high_ref, low_ref, edge_high, edge_low, own_ref, other_ref):
    match(slots_ref, pick_ref, slots_of(place_ref[1], chunk), POINTS)
    inner, edge = pick_ref[:, :INNER], pick_ref[:, INNER:]
    chosen = (
        contract(high_ref[...], inner)
        + contract(low_ref[...], inner)
        + contract(edge_high[...], edge)
        + contract(edge_low[...], edge)
    )
    own_ref[...] = chosen[:SENT, :SLOTS]
    other_ref[...] = chosen[:SENT, SLOTS:]


def rest_kernel(
    chunks, place_ref, high_ref, low_ref, edge_ref, south_ref, north_ref, land_ref, slots_ref, speed_ref, *rest
):
    sent, (pick_ref, fixed_ref, edge_high, edge_low) = rest[:-4], rest[-4:]
    core = place_ref[1]
    fixed_ref[...] = edge_ref[...]
    south_row = land_ref[0:1, :].astype(f32)
    north_row = land_ref[ROWS - 1 : ROWS, :].astype(f32)

    def fix(parity):
        for b in range((BLOCKS + 1) // 2):
            at = slice(b * HALF, (b + 1) * HALF)
            north_going, south_going = 2 * b + parity, 2 * b + 1 - parity
            if north_going < BLOCKS:
                mine = slice(north_going * HALF, (north_going + 1) * HALF)
                speed = jnp.broadcast_to(speed_ref[mine, 2:3], (HALF, COLS))
                fixed_ref[0, mine, :] += speed * south_ref[at, :] * south_row
            if south_going < BLOCKS:
                mine = slice(south_going * HALF, (south_going + 1) * HALF)
                speed = jnp.broadcast_to(speed_ref[mine, 3:4], (HALF, COLS))
                fixed_ref[1, mine, :] -= speed * north_ref[at, :] * north_row

    for parity in (0, 1):
        pl.when(core == parity)(functools.partial(fix, parity))
    for i in range(2):
        at = slice(i * COLS, (i + 1) * COLS)
        edge_high[:, at], edge_low[:, at] = split(fixed_ref[i])

    for n, m in enumerate(chunks):
        own_ref, other_ref = sent[2 * n :][:2]
        choose(place_ref, slots_ref, pick_ref, m, high_ref, low_ref, edge_high, edge_low, own_ref, other_ref)


def rates_kernel(ways_ref, growth_ref, whitecap_ref, *rate_refs):
    frequency, direction = numbered(0, ALL)
    values = (
        look_up(direction, ways_ref[4:5, :]),
        look_up(direction, ways_ref[5:6, :]),
        substep * look_up(frequency, growth_ref[...]),
        substep * look_up(frequency, whitecap_ref[...]),
    )
    for ref, column in zip(rate_refs, values):
        ref[...] = jnp.broadcast_to(column, (ALL, LANES))


def source_kernel(place_ref, own_ref, pair_ref, far_ref, cross_ref, coupling_ref, *rest):
    rate_refs = rest[:4]
    folded = rest[-1].ndim == 3
    out_ref, back_ref, state_ref, rounded_ref, input_ref, *unfolded = rest[-5 - folded :]
    width = state_ref.shape[1]
    arrived = (own_ref, pair_ref, far_ref, cross_ref)
    group = place_ref[0]

    if folded:
        (flat_ref,) = unfolded
        lane = lax.broadcasted_iota(jnp.int32, (FOLDED, LANES), 1)
        for q, ref in enumerate(arrived):
            for j in range(FOLD):
                half, run = divmod(j, BESIDE)
                moved = ref[SENT:, half * LANES : (half + 1) * LANES]
                moved = pltpu.roll(moved, LANES - run * FEW, 1) if run else moved
                flat_ref[q, j * FOLDED : (j + 1) * FOLDED, :] = jnp.where(lane < FEW, moved, 0.0)

    def load(g):
        for q, ref in enumerate(arrived):
            first = (g ^ q) * GROUP
            state_ref[first : first + GROUP, :SLOTS] = ref[:GROUP, :]
            if folded:
                state_ref[first : first + GROUP, SLOTS:] = flat_ref[q, :GROUP, :]

    for g in range(GROUPS):
        pl.when(group == g)(functools.partial(load, g))
    wind = own_ref[GROUP : GROUP + 3, :]
    if folded:
        wind = jnp.concatenate([wind, flat_ref[0, GROUP : GROUP + 3, :]], axis=1)
    speed, cosine, sine = (wind[j : j + 1, :] for j in range(3))

    def wide(ref, at):
        return jnp.concatenate([ref[at, :]] * (width // LANES), axis=1)

    total = jnp.zeros((1, width), f32)
    for start, stop in zip(CUTS[:-1], CUTS[1:]):
        at = slice(start, stop)
        east, north, growth = (wide(ref, at) for ref in rate_refs[:3])
        facing = 0.5 + 0.5 * (east * cosine + north * sine)
        input_ref[at, :] = growth * speed * (facing * facing)
        state = state_ref[at, :]
        rounded_ref[0, at, :] = state.astype(bf16)
        total = total + jnp.sum(state * state, axis=0, keepdims=True)

    def update(at, step, damping):
        transfer = jnp.dot(coupling_ref[at, :], rounded_ref[step % 2], preferred_element_type=f32)
        state = state_ref[at, :]
        whitecap = wide(rate_refs[3], at)
        return state + (substep * transfer + (input_ref[at, :] - whitecap * damping) * state)

    for step in range(SUBSTEPS):
        mean_square = total * (1.0 / ALL)
        damping = mean_square / (1.0 + mean_square)
        total = jnp.zeros((1, width), f32)
        if step < SUBSTEPS - 1:
            for start, stop in zip(CUTS[:-1], CUTS[1:]):
                at = slice(start, stop)
                values = update(at, step, damping)
                state_ref[at, :] = values
                rounded_ref[(step + 1) % 2, at, :] = values.astype(bf16)
                total = total + jnp.sum(values * values, axis=0, keepdims=True)
        else:
            here = (group // 2) * LOWER
            for start, count in ((0, 464), (464, ALL - LOWER - 464)):
                at = pl.ds(pl.multiple_of(here + start, TILE), count)
                state_ref[at, :] = update(at, step, damping)

    def give(g):
        out_ref[:GROUP, :] = state_ref[g * GROUP : (g + 1) * GROUP, :]
        back_ref[:GROUP, :] = state_ref[(g ^ 1) * GROUP : ((g ^ 1) + 1) * GROUP, :]

    for g in range(GROUPS):
        pl.when(group == g)(functools.partial(give, g))


def spread(place_ref, slots_ref, pick_ref, chunks, own, came, add):
    for n, chunk in enumerate(chunks):
        match(slots_ref, pick_ref, slots_of(place_ref[1], chunk), POINTS)
        values = jnp.concatenate([own[n][...], came[n][...]], axis=1)
        high, low = split(values)
        rows = values.shape[1]
        for i in range(ROWS):
            at = slice(i * COLS, (i + 1) * COLS)
            add(
                n,
                i,
                jnp.dot(high, pick_ref[:rows, at], preferred_element_type=f32)
                + jnp.dot(low, pick_ref[:rows, at], preferred_element_type=f32),
            )


def gather_kernel(chunks, more, place_ref, slots_ref, *rest):
    before, rest = (rest[0], rest[1:]) if more else (None, rest)
    count = len(chunks)
    own, came, (sum_ref, pick_ref) = rest[:count], rest[count : 2 * count], rest[2 * count :]

    def add(n, i, values):
        at = slice(i * COLS, (i + 1) * COLS)
        if n:
            sum_ref[:, at] += values
        else:
            sum_ref[:, at] = values + before[:, at] if more else values

    spread(place_ref, slots_ref, pick_ref, chunks, own, came, add)


def lines_of(i, h):
    return pl.ds(h * ROWS + ORDER[i], GROUP, stride=LINES)


def finish_kernel(chunk, place_ref, slots_ref, sum_ref, own_ref, came_ref, out_ref, pick_ref):
    def add(n, i, values):
        at = slice(i * COLS, (i + 1) * COLS)
        values = values[:GROUP] + sum_ref[:GROUP, at]
        for h in range(COLS // LANES):
            out_ref[lines_of(i, h), :] = values[:, h * LANES : (h + 1) * LANES]

    spread(place_ref, slots_ref, pick_ref, (chunk,), (own_ref,), (came_ref,), add)


def add_kernel(chunk, place_ref, slots_ref, sum_ref, own_ref, came_ref, out_ref, pick_ref):
    def add(n, i, values):
        for h in range(COLS // LANES):
            lines = lines_of(i, h)
            out_ref[lines, :] = sum_ref[lines, :] + values[:GROUP, h * LANES : (h + 1) * LANES]

    spread(place_ref, slots_ref, pick_ref, (chunk,), (own_ref,), (came_ref,), add)


def call(kernel, out, flops, scratch=(), scalars=1, inputs=0, unread=0, mib=12, moved=8 * MIB, out_scalars=0):
    return pl.pallas_call(
        kernel,
        out_shape=out,
        in_specs=[SCALAR] * scalars + [WHOLE] * inputs + [UNREAD] * unread,
        out_specs=(SCALAR,) * out_scalars + (WHOLE,) * (len(out) - out_scalars) if isinstance(out, tuple) else WHOLE,
        scratch_shapes=list(scratch),
        compiler_params=pltpu.CompilerParams(vmem_limit_bytes=mib * MIB),
        cost_estimate=pl.CostEstimate(flops=flops, bytes_accessed=moved, transcendentals=0),
    )


def pairs(flip):
    return [(g, g ^ flip) for g in range(GROUPS)]


def ways():
    bearing = (np.arange(ND) + 0.5) * (2.0 * math.pi / ND)
    cosine, sine = np.cos(bearing), np.sin(bearing)
    rows = [np.maximum(cosine, 0), np.minimum(cosine, 0), np.maximum(sine, 0), np.minimum(sine, 0), cosine, sine]
    table = np.zeros((ROWS, LANES), np.float32)
    table[: len(rows), :ND] = rows
    return jnp.asarray(table)


def by_lane(values):
    return jnp.pad(values, (0, LANES - NF))[None, :]


def lined(spectra):
    return spectra.reshape(GROUP, ROWS, COLS // LANES, LANES).swapaxes(1, 2).reshape(GROUP * LINES, LANES)


def on_device(spectra, land_mask, courant, wind_speed, wind_angle, growth, whitecap, coupling):
    group = lax.axis_index("comp")
    place = jnp.stack([group, group % 2]).astype(jnp.int32)

    halo = jax.ShapeDtypeStruct((PACKED, COLS), f32)
    up, down = call(pack_kernel, (halo, halo), 10**6, inputs=2)(place, lined(spectra), land_mask)
    count = lax.axis_size("pts")
    south = lax.ppermute(up, "pts", [(i, i + 1) for i in range(count - 1)])
    north = lax.ppermute(down, "pts", [(i + 1, i) for i in range(count - 1)])

    message = jax.ShapeDtypeStruct((SENT, SLOTS), f32)
    pick = pltpu.VMEM((CHUNK, POINTS), bf16)
    raw = (spectra, land_mask, courant, wind_speed, wind_angle, growth, whitecap)

    def moved_on(raw, after):
        spectra, land_mask, courant, wind_speed, wind_angle, _, _ = raw
        first = jax.ShapeDtypeStruct((SENT_FIRST, SLOTS), f32)
        inner = jax.ShapeDtypeStruct((HELD, INNER), bf16)
        return call(
            advect_kernel,
            (
                jax.ShapeDtypeStruct((1,), jnp.int32),
                jax.ShapeDtypeStruct((ROWS, COLS), f32),
                jax.ShapeDtypeStruct((HELD, LANES), f32),
                inner,
                inner,
                jax.ShapeDtypeStruct((2, HELD, COLS), f32),
                first,
                first,
            ),
            2 * 10**9,
            [pltpu.VMEM((ROWS, COLS), f32), pltpu.VMEM((CHUNK, INNER), bf16), pltpu.VMEM((ROWS, TILE, COLS), f32)],
            inputs=6,
            unread=1,
            mib=16,
            out_scalars=1,
        )(place, lined(spectra), land_mask, by_lane(courant), ways(), wind_speed, wind_angle, after)

    def rest_of(chunks, moved, land_mask, south, north):
        _, slots, speeds, high, low, edge, *_ = moved
        return call(
            functools.partial(rest_kernel, chunks),
            (message,) * (2 * len(chunks)),
            4 * 10**9,
            [
                pick,
                pltpu.VMEM((2, HELD, COLS), f32),
                pltpu.VMEM((HELD, POINTS - INNER), bf16),
                pltpu.VMEM((HELD, POINTS - INNER), bf16),
            ],
            inputs=8,
        )(place, high, low, edge, south, north, land_mask, slots, speeds)

    def rates_of(growth, whitecap):
        return call(rates_kernel, (jax.ShapeDtypeStruct((ALL, LANES), f32),) * 4, 10**6, scalars=0, inputs=3)(
            ways(), by_lane(growth), by_lane(whitecap)
        )

    moved = moved_on(raw, up)
    used, slots = moved[:2]
    messages = list(moved[6:]) + list(rest_of(range(CHUNKS), moved, land_mask, south, north))
    rates = rates_of(growth, whitecap)

    def worked(coupling, rates, own, other, *after):
        folded = own.shape[0] == SENT_FIRST
        width = WIDE if folded else SLOTS
        far = lax.ppermute(own, "comp", pairs(2))
        cross = lax.ppermute(other, "comp", pairs(3))
        pair = lax.ppermute(other, "comp", pairs(1))
        scratch = [pltpu.VMEM((ALL, width), f32), pltpu.VMEM((2, ALL, width), bf16), pltpu.VMEM((ALL, width), f32)]
        out, back = call(
            source_kernel,
            (jax.ShapeDtypeStruct((SENT, width), f32),) * 2,
            4 * 10**9,
            scratch + [pltpu.VMEM((4, HELD, LANES), f32)] * folded,
            inputs=9,
            unread=len(after),
            mib=20 if folded else 18,
        )(place, own, pair, far, cross, coupling, *rates, *after)
        return out, lax.ppermute(back, "comp", pairs(1))

    steps = (None,) + tuple(range(CHUNKS))
    done = []
    after = ()
    sums = jax.ShapeDtypeStruct((SENT, POINTS), f32)
    for n, chunk in enumerate(steps):
        done.append(worked(coupling, rates, *messages[2 * n : 2 * n + 2], *after))
        after = done[-1][:1]
        if n == 0:
            total = call(
                functools.partial(gather_kernel, steps[:1], False),
                sums,
                7 * 10**9,
                [pltpu.VMEM((2 * WIDE, POINTS), bf16)],
                inputs=3,
            )(place, slots, *done[0])
        if n == len(steps) - 2:
            after += (total,)
    total = call(functools.partial(gather_kernel, steps[1:-1], True), sums, 7 * 10**9, [pick], inputs=4)(
        place, slots, total, *done[-2]
    )
    finished = jax.ShapeDtypeStruct((GROUP * LINES, LANES), f32)
    result = call(functools.partial(finish_kernel, steps[-1]), finished, 2 * 10**9, [pick], inputs=4)(
        place, slots, total, *done[-1]
    )

    def one_more(result, raw, coupling, south, north):
        moved = moved_on(raw, south)
        own, other = rest_of((CHUNKS,), moved, raw[1], south, north)
        return call(functools.partial(add_kernel, CHUNKS), finished, 2 * 10**9, [pick], inputs=4)(
            place, moved[1], result, *worked(coupling, rates_of(*raw[-2:]), own, other)
        )

    def no_more(result, *_):
        return result

    result = lax.cond(used[0] > USUAL, one_more, no_more, result, raw, coupling, south, north)
    return result.reshape(GROUP, COLS // LANES, ROWS, LANES).swapaxes(1, 2).reshape(GROUP, ROWS, COLS)


def solution(mesh):
    placed = (
        P("comp", "pts", None),
        P("pts", None),
        P(),
        P("pts", None),
        P("pts", None),
        P(),
        P(),
        P(),
    )
    return jax.shard_map(
        on_device, mesh=mesh, in_specs=placed, out_specs=P("comp", "pts", None), check_vma=False
    )
```

```python
import functools
import math

import jax
import jax.numpy as jnp
from jax import lax
from jax.experimental import pallas as pl
from jax.experimental.pallas import tpu as pltpu
from jax.sharding import PartitionSpec as P
import numpy as np

NF = 50
ND = 36
HALF = ND // 2
SUBSTEPS = 3
substep = 0.5

GROUP = 450
SENT = 456
HELD = 480
GROUPS = 4
ALL = GROUPS * GROUP
BLOCKS = GROUP // HALF
PACKED = (BLOCKS + 1) // 2 * HALF
ROWS = 8
COLS = 256
LANES = 128
LINES = ROWS * COLS // LANES
ORDER = (1, 2, 3, 4, 5, 6, 0, 7)
INNER = 6 * COLS
POINTS = ROWS * COLS
SLOTS = 256
CHUNK = 2 * SLOTS
BESIDE = 3
FOLD = 2 * BESIDE
FEW = LANES // BESIDE
FOLDED = HELD // FOLD
MOST = SLOTS + FEW
WIDE = SLOTS + LANES
FIRST = 2 * MOST
CHUNKS = 2
USUAL = FIRST + CHUNKS * CHUNK
SENT_FIRST = SENT + FOLDED
TILE = 16
LATE_FAR = True
CUTS = (0, 464, 928, 1392, ALL)
LOWER = 896
MIB = 1 << 20
f32 = jnp.float32
bf16 = jnp.bfloat16

WHOLE = pl.BlockSpec(memory_space=pltpu.VMEM)
SCALAR = pl.BlockSpec(memory_space=pltpu.SMEM)
ANYWHERE = pl.BlockSpec(memory_space=pl.ANY)


def grid_row(ref, first, count, y):
    halves = [ref[pl.ds(first * LINES + h * ROWS + y, count, stride=LINES), :] for h in range(COLS // LANES)]
    return jnp.concatenate(halves, axis=1)


def split(values):
    high = values.astype(bf16)
    return high, (values - high.astype(f32)).astype(bf16)


def in_order(values):
    return jnp.concatenate([values[y : y + 1] for y in ORDER], axis=0)


def numbered(first, count):
    k = (lax.broadcasted_iota(jnp.int32, (count, LANES), 0) + first).astype(f32)
    frequency = jnp.floor((k + 0.5) * (1.0 / ND))
    return frequency, k - ND * frequency


def look_up(index, table):
    lane = lax.broadcasted_iota(jnp.int32, index.shape, 1).astype(f32)
    return jnp.sum(jnp.where(index == lane, table, 0.0), axis=1, keepdims=True)


def columns(values, count):
    lane = lax.broadcasted_iota(jnp.int32, (count, LANES), 1)
    return sum(jnp.where(lane == i, column, 0.0) for i, column in enumerate(values))


def pack_kernel(place_ref, spec_ref, land_ref, up_ref, down_ref):
    core = place_ref[1]
    south_row = land_ref[0:1, :].astype(f32)
    north_row = land_ref[ROWS - 1 : ROWS, :].astype(f32)

    def pack(parity):
        for b in range((BLOCKS + 1) // 2):
            north_going = min(2 * b + parity, BLOCKS - 1) * HALF
            south_going = min(2 * b + 1 - parity, BLOCKS - 1) * HALF
            at = slice(b * HALF, (b + 1) * HALF)
            up_ref[at, :] = grid_row(spec_ref, north_going, HALF, ROWS - 1) * north_row
            down_ref[at, :] = grid_row(spec_ref, south_going, HALF, 0) * south_row

    for parity in (0, 1):
        pl.when(core == parity)(functools.partial(pack, parity))


def match(slots_ref, pick_ref, number, i):
    hit = slots_ref[pl.ds(i, 1), :] == number.astype(f32)
    pick_ref[: number.shape[0], :] = jnp.where(hit, 1.0, 0.0).astype(bf16)


def slots_of(core, chunk, sides=(0, 1), few=False):
    count = LANES if few else WIDE if chunk is None else SLOTS
    line = lax.broadcasted_iota(jnp.int32, (len(sides) * count, COLS), 0)
    if len(sides) == 1:
        side, place = sides[0], line
    else:
        side = jnp.where(line < count, 0, 1)
        place = line - count * side
    side = jnp.bitwise_xor(core, side)
    if few:
        return jnp.where(place < FEW, side * MOST + SLOTS + place, -2)
    if chunk is None:
        return jnp.where(place < MOST, side * MOST + place, -2)
    return FIRST + chunk * CHUNK + side * SLOTS + place


def when_in(bounds_ref, i, chunk, run, otherwise=None):
    first = 0 if chunk is None else FIRST + chunk * CHUNK
    stop = FIRST if chunk is None else first + CHUNK
    here = (bounds_ref[2 * i] < stop) & (bounds_ref[2 * i + 1] > first)
    pl.when(here)(run)
    if otherwise is not None:
        pl.when(jnp.logical_not(here))(otherwise)


def contract(a, b):
    return lax.dot_general(a, b, (((1,), (1,)), ((), ())), preferred_element_type=f32)


def advect_kernel(
    place_ref, spec_ref, land_ref, courant_ref, ways_ref, wind_ref, angle_ref, after_ref,
    used_ref, bounds_ref, slots_ref, speed_ref, high_ref, low_ref, edge_ref, *rest,
):
    sent, (sea_ref, pick_ref, tail_ref) = rest[:-3], rest[-3:]
    group, core = place_ref[0], place_ref[1]
    sea = in_order(land_ref[...]).astype(f32)
    sea_ref[...] = sea

    ramp = [lax.broadcasted_iota(jnp.int32, (COLS, COLS), axis) for axis in (0, 1)]
    upper = jnp.where(ramp[0] <= ramp[1], 1.0, 0.0).astype(bf16)
    running = jnp.dot(sea.astype(bf16), upper, preferred_element_type=f32)
    before = jnp.zeros((1, 1), f32)
    for i in range(ROWS):
        if i == 6:
            before = jnp.maximum(before, 1.0 * FIRST)
        slots_ref[i : i + 1, :] = jnp.where(
            sea[i : i + 1] > 0.0, running[i : i + 1] - 1.0 + before, -1.0
        )
        bounds_ref[2 * i] = jnp.max(before).astype(jnp.int32)
        before = before + running[i : i + 1, COLS - 1 :]
        bounds_ref[2 * i + 1] = jnp.max(before).astype(jnp.int32)
    used_ref[0] = bounds_ref[2 * ROWS - 1]

    frequency, direction = numbered(group * GROUP, HELD)
    speed = look_up(frequency, courant_ref[...])
    across, along = (speed * look_up(direction, ways_ref[i : i + 1, :]) for i in range(2))
    signs = [look_up(direction, ways_ref[i : i + 1, :]) for i in (2, 3)]
    speed_ref[...] = columns([across, along, 1.0 - across - along] + signs, HELD)

    lane = lax.broadcasted_iota(jnp.int32, (1, COLS), 1)
    not_first = jnp.where(lane > 0, 1.0, 0.0)
    not_last = jnp.where(lane < COLS - 1, 1.0, 0.0)

    def advect(first, count, store):
        speeds = [
            jnp.broadcast_to(speed_ref[pl.ds(first, count), i : i + 1], (count, COLS)) for i in range(5)
        ]
        across, along, stay = speeds[:3]
        eastward, northward = (values > 0.5 for values in speeds[3:])

        halves = [jnp.swapaxes(spec_ref[pl.ds(first, count), h], 0, 1) for h in range(COLS // LANES)]

        def row(y):
            i = ORDER.index(y)
            return jnp.concatenate([half[y] for half in halves], axis=1) * sea_ref[i : i + 1, :]

        before, here = jnp.zeros((count, COLS), f32), row(0)
        for y in range(ROWS):
            after = row(y + 1) if y < ROWS - 1 else jnp.zeros((count, COLS), f32)
            west = pltpu.roll(here, 1, 1) * not_first
            east = pltpu.roll(here, COLS - 1, 1) * not_last
            moved = stay * here + across * jnp.where(eastward, west, east)
            moved = moved + along * jnp.where(northward, before, after)
            i = ORDER.index(y)
            store(i, moved * sea_ref[i : i + 1, :])
            before, here = here, after

    def keep(first):
        def store(i, values):
            if i < 6:
                at = slice(i * COLS, (i + 1) * COLS)
                high, low = split(values)
                high_ref[pl.ds(first, TILE), at] = high
                low_ref[pl.ds(first, TILE), at] = low
            else:
                edge_ref[i - 6, pl.ds(first, TILE), :] = values

        return store

    def step(t, carry):
        first = pl.multiple_of(t * TILE, TILE)
        advect(first, TILE, keep(first))
        return carry

    full = GROUP // TILE
    lax.fori_loop(0, full, step, 0)
    last = full * TILE
    left = GROUP - last
    tail_ref[...] = jnp.zeros_like(tail_ref)
    rest_of = slice(last + TILE, HELD)
    for ref in (high_ref, low_ref):
        ref[rest_of, :] = jnp.zeros((HELD - last - TILE, INNER), bf16)
    edge_ref[:, rest_of, :] = jnp.zeros((2, HELD - last - TILE, COLS), f32)

    def keep_tail(i, values):
        tail_ref[i, 0:left, :] = values

    advect(last, left, keep_tail)
    angle = in_order(angle_ref[...])
    for j, values in enumerate((in_order(wind_ref[...]), jnp.cos(angle), jnp.sin(angle))):
        for i in range(ROWS):
            tail_ref[i, left + j : left + j + 1, :] = values[i : i + 1]
    for i in range(ROWS):
        if i < 6:
            at = slice(i * COLS, (i + 1) * COLS)
            high, low = split(tail_ref[i])
            high_ref[last : last + TILE, at] = high
            low_ref[last : last + TILE, at] = low
        else:
            edge_ref[i - 6, last : last + TILE, :] = tail_ref[i]

    def picked(number):
        rows = number.shape[0]
        for i in range(6):
            match(slots_ref, pick_ref.at[:rows, i * COLS : (i + 1) * COLS], number, i)
        pick = pick_ref[:rows, :]
        return contract(high_ref[...], pick) + contract(low_ref[...], pick)

    few = picked(slots_of(core, None, few=True))
    for i, ref in enumerate(sent):
        for half in range(FOLD // BESIDE):
            first = [(half * BESIDE + r) * FOLDED for r in range(BESIDE)]
            runs = [few[n : n + FOLDED, i * LANES : (i + 1) * LANES] for n in first]
            runs = [pltpu.roll(values, r * FEW, 1) if r else values for r, values in enumerate(runs)]
            ref[SENT:, half * LANES : (half + 1) * LANES] = sum(runs)
    line = lax.broadcasted_iota(jnp.int32, (CHUNK, COLS), 0)
    side = jnp.where(line < SLOTS, 0, 1)
    chosen = picked(jnp.bitwise_xor(core, side) * MOST + line - SLOTS * side)
    for i, ref in enumerate(sent):
        ref[:SENT, :] = chosen[:SENT, i * SLOTS : (i + 1) * SLOTS]


def choose(place_ref, bounds_ref, slots_ref, pick_ref, sum_ref, chunk, parts, own_ref, other_ref):
    sum_ref[...] = jnp.zeros_like(sum_ref)
    for i in range(ROWS):

        def add(i=i):
            match(slots_ref, pick_ref, slots_of(place_ref[1], chunk), i)
            high, low = parts(i)
            sum_ref[...] += contract(high, pick_ref[...]) + contract(low, pick_ref[...])

        when_in(bounds_ref, i, chunk, add)
    own_ref[...] = sum_ref[:SENT, :SLOTS]
    other_ref[...] = sum_ref[:SENT, SLOTS:]


def rest_kernel(
    chunks, place_ref, bounds_ref, high_ref, low_ref, edge_ref, south_ref, north_ref, land_ref, slots_ref, speed_ref, *rest
):
    sent, (pick_ref, sum_ref, fixed_ref, edge_high, edge_low) = rest[:-5], rest[-5:]
    core = place_ref[1]
    fixed_ref[...] = edge_ref[...]
    south_row = land_ref[0:1, :].astype(f32)
    north_row = land_ref[ROWS - 1 : ROWS, :].astype(f32)

    def fix(parity):
        for b in range((BLOCKS + 1) // 2):
            at = slice(b * HALF, (b + 1) * HALF)
            north_going, south_going = 2 * b + parity, 2 * b + 1 - parity
            if north_going < BLOCKS:
                mine = slice(north_going * HALF, (north_going + 1) * HALF)
                speed = jnp.broadcast_to(speed_ref[mine, 1:2], (HALF, COLS))
                fixed_ref[0, mine, :] += speed * south_ref[at, :] * south_row
            if south_going < BLOCKS:
                mine = slice(south_going * HALF, (south_going + 1) * HALF)
                speed = jnp.broadcast_to(speed_ref[mine, 1:2], (HALF, COLS))
                fixed_ref[1, mine, :] += speed * north_ref[at, :] * north_row

    for parity in (0, 1):
        pl.when(core == parity)(functools.partial(fix, parity))
    for i in range(2):
        at = slice(i * COLS, (i + 1) * COLS)
        edge_high[:, at], edge_low[:, at] = split(fixed_ref[i])

    def parts(i):
        if i < 6:
            return high_ref[:, i * COLS : (i + 1) * COLS], low_ref[:, i * COLS : (i + 1) * COLS]
        return edge_high[:, (i - 6) * COLS : (i - 5) * COLS], edge_low[:, (i - 6) * COLS : (i - 5) * COLS]

    for n, m in enumerate(chunks):
        choose(place_ref, bounds_ref, slots_ref, pick_ref, sum_ref, m, parts, *sent[2 * n : 2 * n + 2])


def rates_kernel(ways_ref, growth_ref, whitecap_ref, *rate_refs):
    frequency, direction = numbered(0, ALL)
    values = (
        look_up(direction, ways_ref[4:5, :]),
        look_up(direction, ways_ref[5:6, :]),
        substep * look_up(frequency, growth_ref[...]),
        substep * look_up(frequency, whitecap_ref[...]),
    )
    for ref, column in zip(rate_refs, values):
        ref[...] = jnp.broadcast_to(column, (ALL, LANES))


def source_kernel(place_ref, own_ref, pair_ref, far_ref, cross_ref, coupling_ref, *rest):
    rate_refs = rest[:4]
    folded = rest[-1].ndim == 3
    out_ref, back_ref, state_ref, rounded_ref, input_ref, *unfolded = rest[-5 - folded :]
    width = state_ref.shape[1]
    arrived = (own_ref, pair_ref, far_ref, cross_ref)
    group = place_ref[0]

    if folded:
        (flat_ref,) = unfolded
        lane = lax.broadcasted_iota(jnp.int32, (FOLDED, LANES), 1)
        for q, ref in enumerate(arrived):
            for j in range(FOLD):
                half, run = divmod(j, BESIDE)
                moved = ref[SENT:, half * LANES : (half + 1) * LANES]
                moved = pltpu.roll(moved, LANES - run * FEW, 1) if run else moved
                flat_ref[q, j * FOLDED : (j + 1) * FOLDED, :] = jnp.where(lane < FEW, moved, 0.0)

    def load(g):
        for q, ref in enumerate(arrived):
            first = (g ^ q) * GROUP
            state_ref[first : first + GROUP, :SLOTS] = ref[:GROUP, :]
            if folded:
                state_ref[first : first + GROUP, SLOTS:] = flat_ref[q, :GROUP, :]

    for g in range(GROUPS):
        pl.when(group == g)(functools.partial(load, g))
    wind = own_ref[GROUP : GROUP + 3, :]
    if folded:
        wind = jnp.concatenate([wind, flat_ref[0, GROUP : GROUP + 3, :]], axis=1)
    total = set_up(rate_refs, wind, state_ref, rounded_ref.at[0], input_ref)

    def transfer(at):
        return jnp.dot(coupling_ref[at, :], rounded_ref[0], preferred_element_type=f32)

    substeps(group, total, transfer, coupling_ref, rate_refs[3], input_ref, state_ref, rounded_ref, out_ref, back_ref)


def wide(ref, at, width):
    return jnp.concatenate([ref[at, :]] * (width // LANES), axis=1)


def blocks():
    return [slice(start, stop) for start, stop in zip(CUTS[:-1], CUTS[1:])]


def set_up(rate_refs, wind, state_ref, rounded_ref, input_ref):
    width = state_ref.shape[1]
    speed, cosine, sine = (wind[j : j + 1, :] for j in range(3))
    total = jnp.zeros((1, width), f32)
    for at in blocks():
        east, north, growth = (wide(ref, at, width) for ref in rate_refs[:3])
        facing = 0.5 + 0.5 * (east * cosine + north * sine)
        input_ref[at, :] = growth * speed * (facing * facing)
        state = state_ref[at, :]
        rounded_ref[at, :] = state.astype(bf16)
        total = total + jnp.sum(state * state, axis=0, keepdims=True)
    return total


def substeps(group, total, first_transfer, coupling_ref, whitecap_ref, input_ref, state_ref, rounded_ref, out_ref, back_ref):
    width = state_ref.shape[1]

    def update(at, step, damping):
        if step:
            transfer = jnp.dot(coupling_ref[at, :], rounded_ref[step % 2], preferred_element_type=f32)
        else:
            transfer = first_transfer(at)
        state = state_ref[at, :]
        whitecap = wide(whitecap_ref, at, width)
        return state + (substep * transfer + (input_ref[at, :] - whitecap * damping) * state)

    for step in range(SUBSTEPS):
        mean_square = total * (1.0 / ALL)
        damping = mean_square / (1.0 + mean_square)
        total = jnp.zeros((1, width), f32)
        if step < SUBSTEPS - 1:
            for at in blocks():
                values = update(at, step, damping)
                state_ref[at, :] = values
                rounded_ref[(step + 1) % 2, at, :] = values.astype(bf16)
                total = total + jnp.sum(values * values, axis=0, keepdims=True)
        else:
            here = (group // 2) * LOWER
            for start, count in ((0, 464), (464, ALL - LOWER - 464)):
                at = pl.ds(pl.multiple_of(here + start, TILE), count)
                state_ref[at, :] = update(at, step, damping)

    def give(g):
        out_ref[:GROUP, :] = state_ref[g * GROUP : (g + 1) * GROUP, :]
        back_ref[:GROUP, :] = state_ref[(g ^ 1) * GROUP : ((g ^ 1) + 1) * GROUP, :]

    for g in range(GROUPS):
        pl.when(group == g)(functools.partial(give, g))


def ready_kernel(late, place_ref, *rest):
    arrived, coupling_ref, rate_refs = rest[:3], rest[3], rest[4:8]
    state_ref, input_ref, transfer_ref, total_ref, rounded_ref = rest[-5:]
    group = place_ref[0]

    def load(g):
        for q, ref in zip([q for q in range(GROUPS) if q != late], arrived):
            first = (g ^ q) * GROUP
            state_ref[first : first + GROUP, :] = ref[:GROUP, :]
        first = (g ^ late) * GROUP
        state_ref[first : first + GROUP, :] = jnp.zeros((GROUP, SLOTS), f32)

    for g in range(GROUPS):
        pl.when(group == g)(functools.partial(load, g))
    total = set_up(rate_refs, arrived[0][GROUP : GROUP + 3, :], state_ref, rounded_ref, input_ref)
    total_ref[...] = jnp.broadcast_to(total, total_ref.shape)
    for at in blocks():
        transfer_ref[at, :] = jnp.dot(coupling_ref[at, :], rounded_ref[...], preferred_element_type=f32)


def last_kernel(late, place_ref, *rest):
    came_ref, before_ref, input_ref, partial_ref, total_ref, coupling_ref, whitecap_ref = rest[:7]
    out_ref, back_ref, state_ref, rounded_ref, transfer_ref, window_ref = rest[-6:]
    group = place_ref[0]
    came = came_ref[:GROUP, :]
    total = total_ref[0:1, :] + jnp.sum(came * came, axis=0, keepdims=True)
    state_ref[...] = before_ref[...]

    def load(g):
        first = g * GROUP
        start, stop = first // LANES * LANES, min(-(-(first + GROUP) // LANES) * LANES, ALL)
        values = came_ref[:GROUP, :]
        state_ref[first : first + GROUP, :] = values
        window_ref[...] = jnp.zeros_like(window_ref)
        window_ref[first - start : first - start + GROUP, :] = values
        rounded = window_ref[: stop - start, :].astype(bf16)
        for at in blocks():
            transfer_ref[at, :] = partial_ref[at, :] + jnp.dot(
                coupling_ref[at, start:stop], rounded, preferred_element_type=f32
            )

    for g in range(GROUPS):
        pl.when(group == g ^ late)(functools.partial(load, g))
    substeps(
        group, total, lambda at: transfer_ref[at, :], coupling_ref, whitecap_ref, input_ref, state_ref, rounded_ref,
        out_ref, back_ref,
    )


def spread(place_ref, bounds_ref, slots_ref, pick_ref, parts_ref, chunk, sides, values, add, keep=None):
    number = slots_of(place_ref[1], chunk, sides)
    width = number.shape[0]
    for n, ref in enumerate(values):
        at = slice(n * ref.shape[1], (n + 1) * ref.shape[1])
        parts_ref[:SENT, at], parts_ref[SENT:, at] = split(ref[...])

    def grid_row(i, carry):
        def run():
            match(slots_ref, pick_ref.at[:width], number, i)
            both = jnp.dot(parts_ref[:, :width], pick_ref[:width, :], preferred_element_type=f32)
            add(i, both[:SENT] + both[SENT:])

        when_in(bounds_ref, i, chunk, run, keep and functools.partial(keep, i))
        return carry

    lax.fori_loop(0, ROWS, grid_row, 0)


def lanes_of(i):
    return pl.ds(pl.multiple_of(i * COLS, COLS), COLS)


def gather(items, refs, before_ref, sum_ref, pick_ref, parts_ref):
    scalars, slots_ref, values = refs[:2], refs[2], refs[3:]
    for n, (chunk, sides) in enumerate(items):
        own, values = values[: len(sides)], values[len(sides) :]

        def add(i, more, n=n):
            at = lanes_of(i)
            if n:
                sum_ref[:, at] += more
            else:
                sum_ref[:, at] = more if before_ref is None else before_ref[:, at] + more

        def keep(i):
            at = lanes_of(i)
            sum_ref[:, at] = jnp.zeros((SENT, COLS), f32) if before_ref is None else before_ref[:, at]

        spread(*scalars, slots_ref, pick_ref, parts_ref, chunk, sides, own, add, None if n else keep)


def gather_kernel(items, more, *refs):
    refs, (sum_ref, pick_ref, parts_ref) = refs[:-3], refs[-3:]
    refs, before_ref = (refs[:-1], refs[-1]) if more else (refs, None)
    gather(items, refs, before_ref, sum_ref, pick_ref, parts_ref)


def lines_of(i, h):
    y = jnp.where(i < 6, i + 1, jnp.where(i == 6, 0, ROWS - 1))
    return pl.ds(h * ROWS + y, GROUP, stride=LINES)


def finish_kernel(chunk, place_ref, bounds_ref, slots_ref, came_ref, sum_ref, out_ref, pick_ref, parts_ref):
    def keep(i, values=None):
        at = lanes_of(i)
        total = sum_ref[:GROUP, at]
        total = total if values is None else total + values[:GROUP]
        for h in range(COLS // LANES):
            out_ref[lines_of(i, h), :] = total[:, h * LANES : (h + 1) * LANES]

    spread(place_ref, bounds_ref, slots_ref, pick_ref, parts_ref, chunk, (1,), (came_ref,), keep, keep)


def add_kernel(chunk, place_ref, bounds_ref, slots_ref, own_ref, came_ref, sum_ref, out_ref, pick_ref, parts_ref):
    def keep(i, values=None):
        for h in range(COLS // LANES):
            at = lines_of(i, h)
            total = sum_ref[at, :]
            out_ref[at, :] = total if values is None else total + values[:GROUP, h * LANES : (h + 1) * LANES]

    spread(place_ref, bounds_ref, slots_ref, pick_ref, parts_ref, chunk, (0, 1), (own_ref, came_ref), keep, keep)


def call(kernel, out, flops, scratch=(), scalars=1, inputs=0, unread=0, mib=12, moved=8 * MIB, out_scalars=0):
    return pl.pallas_call(
        kernel,
        out_shape=out,
        in_specs=[SCALAR] * scalars + [WHOLE] * inputs + [ANYWHERE] * unread,
        out_specs=(SCALAR,) * out_scalars + (WHOLE,) * (len(out) - out_scalars) if isinstance(out, tuple) else WHOLE,
        scratch_shapes=list(scratch),
        compiler_params=pltpu.CompilerParams(vmem_limit_bytes=mib * MIB),
        cost_estimate=pl.CostEstimate(flops=flops, bytes_accessed=moved, transcendentals=0),
    )


def pairs(flip):
    return [(g, g ^ flip) for g in range(GROUPS)]


def ways():
    bearing = (np.arange(ND) + 0.5) * (2.0 * math.pi / ND)
    cosine, sine = np.cos(bearing), np.sin(bearing)
    rows = [np.abs(cosine), np.abs(sine), cosine > 0, sine > 0, cosine, sine]
    table = np.zeros((ROWS, LANES), np.float32)
    table[: len(rows), :ND] = rows
    return jnp.asarray(table)


def by_lane(values):
    return jnp.pad(values, (0, LANES - NF))[None, :]


def tiled(spectra):
    return spectra.reshape(GROUP, ROWS, COLS // LANES, LANES).swapaxes(1, 2)


def on_device(spectra, land_mask, courant, wind_speed, wind_angle, growth, whitecap, coupling):
    group = lax.axis_index("comp")
    place = jnp.stack([group, group % 2]).astype(jnp.int32)

    halo = jax.ShapeDtypeStruct((PACKED, COLS), f32)
    up, down = call(pack_kernel, (halo, halo), 10**6, inputs=2)(place, tiled(spectra).reshape(GROUP * LINES, LANES), land_mask)
    count = lax.axis_size("pts")
    south = lax.ppermute(up, "pts", [(i, i + 1) for i in range(count - 1)])
    north = lax.ppermute(down, "pts", [(i + 1, i) for i in range(count - 1)])

    message = jax.ShapeDtypeStruct((SENT, SLOTS), f32)
    pick = pltpu.VMEM((CHUNK, COLS), bf16)
    raw = (spectra, land_mask, courant, wind_speed, wind_angle, growth, whitecap)

    def moved_on(raw, after):
        spectra, land_mask, courant, wind_speed, wind_angle, _, _ = raw
        first = jax.ShapeDtypeStruct((SENT_FIRST, SLOTS), f32)
        inner = jax.ShapeDtypeStruct((HELD, INNER), bf16)
        return call(
            advect_kernel,
            (
                jax.ShapeDtypeStruct((1,), jnp.int32),
                jax.ShapeDtypeStruct((2 * ROWS,), jnp.int32),
                jax.ShapeDtypeStruct((ROWS, COLS), f32),
                jax.ShapeDtypeStruct((HELD, LANES), f32),
                inner,
                inner,
                jax.ShapeDtypeStruct((2, HELD, COLS), f32),
                first,
                first,
            ),
            2 * 10**9,
            [
                pltpu.VMEM((ROWS, COLS), f32),
                pltpu.VMEM((CHUNK, INNER), bf16),
                pltpu.VMEM((ROWS, TILE, COLS), f32),
            ],
            inputs=6,
            unread=1,
            mib=16,
            out_scalars=2,
        )(place, tiled(spectra), land_mask, by_lane(courant), ways(), wind_speed, wind_angle, after)

    def rest_of(chunks, moved, land_mask, south, north):
        _, bounds, slots, speeds, high, low, edge, *_ = moved
        return call(
            functools.partial(rest_kernel, chunks),
            (message,) * (2 * len(chunks)),
            4 * 10**9,
            [
                pick,
                pltpu.VMEM((HELD, CHUNK), f32),
                pltpu.VMEM((2, HELD, COLS), f32),
                pltpu.VMEM((HELD, POINTS - INNER), bf16),
                pltpu.VMEM((HELD, POINTS - INNER), bf16),
            ],
            scalars=2,
            inputs=8,
        )(place, bounds, high, low, edge, south, north, land_mask, slots, speeds)

    def rates_of(growth, whitecap):
        return call(rates_kernel, (jax.ShapeDtypeStruct((ALL, LANES), f32),) * 4, 10**6, scalars=0, inputs=3)(
            ways(), by_lane(growth), by_lane(whitecap)
        )

    moved = moved_on(raw, up)
    used, bounds, slots = moved[:3]
    messages = list(moved[7:]) + list(rest_of(range(CHUNKS), moved, land_mask, south, north))
    rates = rates_of(growth, whitecap)

    def worked(coupling, rates, own, other, pair, *after):
        folded = own.shape[0] == SENT_FIRST
        width = WIDE if folded else SLOTS
        far = lax.ppermute(own, "comp", pairs(2))
        cross = lax.ppermute(other, "comp", pairs(3))
        scratch = [pltpu.VMEM((ALL, width), f32), pltpu.VMEM((2, ALL, width), bf16), pltpu.VMEM((ALL, width), f32)]
        out, back = call(
            source_kernel,
            (jax.ShapeDtypeStruct((SENT, width), f32),) * 2,
            4 * 10**9,
            scratch + [pltpu.VMEM((4, HELD, LANES), f32)] * folded,
            inputs=9,
            unread=len(after),
            mib=20 if folded else 18,
        )(place, own, pair, far, cross, coupling, *rates, *after)
        return out, lax.ppermute(back, "comp", pairs(1))

    def worked_late(coupling, rates, own, other, pair, after):
        cross = lax.ppermute(other, "comp", pairs(3))
        far = lax.ppermute(own, "comp", pairs(2))
        whole = jax.ShapeDtypeStruct((ALL, SLOTS), f32)
        late = 2 if LATE_FAR else 3
        last, near = (far, cross) if LATE_FAR else (cross, far)
        made = call(
            functools.partial(ready_kernel, late),
            (whole, whole, whole, jax.ShapeDtypeStruct((ROWS, SLOTS), f32)),
            10**9,
            [pltpu.VMEM((ALL, SLOTS), bf16)],
            inputs=8,
            unread=1,
            mib=20,
        )(place, own, pair, near, coupling, *rates, after)
        window = 5 * LANES
        out, back = call(
            functools.partial(last_kernel, late),
            (message, message),
            10**9,
            [
                pltpu.VMEM((ALL, SLOTS), f32),
                pltpu.VMEM((2, ALL, SLOTS), bf16),
                pltpu.VMEM((ALL, SLOTS), f32),
                pltpu.VMEM((window, SLOTS), f32),
            ],
            inputs=7,
            mib=22,
        )(place, last, *made, coupling, rates[3])
        return out, lax.ppermute(back, "comp", pairs(1))

    def spread_call(kernel, items, out, bounds, slots, values, before=()):
        width = max((WIDE if chunk is None else SLOTS) * len(sides) for chunk, sides in items)
        scratch = [pltpu.VMEM((width, COLS), bf16), pltpu.VMEM((2 * SENT, width), bf16)]
        if kernel is gather_kernel:
            kernel = functools.partial(kernel, items, bool(before))
        else:
            kernel = functools.partial(kernel, items[0][0])
        count = 1 + len(values) + len(before)
        return call(kernel, out, 4 * 10**9, scratch, scalars=2, inputs=count)(
            place, bounds, slots, *values, *before
        )

    sums = jax.ShapeDtypeStruct((SENT, POINTS), f32)
    finished = jax.ShapeDtypeStruct((GROUP * LINES, LANES), f32)
    pair = [lax.ppermute(other, "comp", pairs(1)) for other in messages[1::2]]
    first_out, first_came = worked(coupling, rates, *messages[:2], pair[0], pair[1])
    next_out, next_came = worked(coupling, rates, *messages[2:4], pair[1], first_out, pair[2])
    total = spread_call(gather_kernel, ((None, (0, 1)),), sums, bounds, slots, (first_out, first_came))
    total = spread_call(gather_kernel, ((0, (0,)),), sums, bounds, slots, (next_out,), (total,))
    last_out, last_came = worked_late(coupling, rates, *messages[4:6], pair[2], total)
    items = ((0, (1,)), (1, (0,)))
    total = spread_call(gather_kernel, items, sums, bounds, slots, (next_came, last_out), (total,))
    result = spread_call(finish_kernel, ((1, (1,)),), finished, bounds, slots, (last_came,), (total,))

    def one_more(result, raw, coupling, south, north):
        moved = moved_on(raw, south)
        own, other = rest_of((CHUNKS,), moved, raw[1], south, north)
        out, came = worked(coupling, rates_of(*raw[-2:]), own, other, lax.ppermute(other, "comp", pairs(1)))
        return spread_call(add_kernel, ((CHUNKS, (0, 1)),), finished, *moved[1:3], (out, came), (result,))

    def no_more(result, *_):
        return result

    result = lax.cond(used[0] > USUAL, one_more, no_more, result, raw, coupling, south, north)
    return result.reshape(GROUP, COLS // LANES, ROWS, LANES).swapaxes(1, 2).reshape(GROUP, ROWS, COLS)


def solution(mesh):
    placed = (
        P("comp", "pts", None),
        P("pts", None),
        P(),
        P("pts", None),
        P("pts", None),
        P(),
        P(),
        P(),
    )
    return jax.shard_map(
        on_device, mesh=mesh, in_specs=placed, out_specs=P("comp", "pts", None), check_vma=False
    )
```

```python
import functools
import math

import jax
import jax.numpy as jnp
from jax import lax
from jax.experimental import pallas as pl
from jax.experimental.pallas import tpu as pltpu
from jax.sharding import PartitionSpec as P
import numpy as np

NF = 50
ND = 36
HALF = ND // 2
SUBSTEPS = 3
substep = 0.5

GROUP = 450
SENT = 456
HELD = 480
GROUPS = 4
ALL = GROUPS * GROUP
BLOCKS = GROUP // HALF
PACKED = (BLOCKS + 1) // 2 * HALF
ROWS = 8
COLS = 256
LANES = 128
LINES = ROWS * COLS // LANES
ORDER = (1, 2, 3, 4, 5, 6, 0, 7)
INNER = 6 * COLS
POINTS = ROWS * COLS
SLOTS = 256
CHUNK = 2 * SLOTS
BESIDE = 3
FOLD = 2 * BESIDE
FEW = LANES // BESIDE
FOLDED = HELD // FOLD
MOST = SLOTS + FEW
WIDE = SLOTS + LANES
FIRST = 2 * MOST
CHUNKS = 2
USUAL = FIRST + CHUNKS * CHUNK
SENT_FIRST = SENT + FOLDED
TILE = 16
LATE_FAR = True
CUTS = (0, 464, 928, 1392, ALL)
LOWER = 896
MIB = 1 << 20
f32 = jnp.float32
bf16 = jnp.bfloat16

WHOLE = pl.BlockSpec(memory_space=pltpu.VMEM)
SCALAR = pl.BlockSpec(memory_space=pltpu.SMEM)
ANYWHERE = pl.BlockSpec(memory_space=pl.ANY)


def grid_row(ref, first, count, y):
    halves = [ref[pl.ds(first * LINES + h * ROWS + y, count, stride=LINES), :] for h in range(COLS // LANES)]
    return jnp.concatenate(halves, axis=1)


def split(values):
    high = values.astype(bf16)
    return high, (values - high.astype(f32)).astype(bf16)


def in_order(values):
    return jnp.concatenate([values[y : y + 1] for y in ORDER], axis=0)


def numbered(first, count):
    k = (lax.broadcasted_iota(jnp.int32, (count, LANES), 0) + first).astype(f32)
    frequency = jnp.floor((k + 0.5) * (1.0 / ND))
    return frequency, k - ND * frequency


def look_up(index, table):
    lane = lax.broadcasted_iota(jnp.int32, index.shape, 1).astype(f32)
    return jnp.sum(jnp.where(index == lane, table, 0.0), axis=1, keepdims=True)


def columns(values, count):
    lane = lax.broadcasted_iota(jnp.int32, (count, LANES), 1)
    return sum(jnp.where(lane == i, column, 0.0) for i, column in enumerate(values))


def pack_kernel(place_ref, spec_ref, land_ref, up_ref, down_ref):
    core = place_ref[1]
    south_row = land_ref[0:1, :].astype(f32)
    north_row = land_ref[ROWS - 1 : ROWS, :].astype(f32)

    def pack(parity):
        for b in range((BLOCKS + 1) // 2):
            north_going = min(2 * b + parity, BLOCKS - 1) * HALF
            south_going = min(2 * b + 1 - parity, BLOCKS - 1) * HALF
            at = slice(b * HALF, (b + 1) * HALF)
            up_ref[at, :] = grid_row(spec_ref, north_going, HALF, ROWS - 1) * north_row
            down_ref[at, :] = grid_row(spec_ref, south_going, HALF, 0) * south_row

    for parity in (0, 1):
        pl.when(core == parity)(functools.partial(pack, parity))


def match(slots_ref, pick_ref, number, i):
    hit = slots_ref[pl.ds(i, 1), :] == number.astype(f32)
    pick_ref[: number.shape[0], :] = jnp.where(hit, 1.0, 0.0).astype(bf16)


def slots_of(core, chunk, sides=(0, 1), few=False):
    count = LANES if few else WIDE if chunk is None else SLOTS
    line = lax.broadcasted_iota(jnp.int32, (len(sides) * count, COLS), 0)
    if len(sides) == 1:
        side, place = sides[0], line
    else:
        side = jnp.where(line < count, 0, 1)
        place = line - count * side
    side = jnp.bitwise_xor(core, side)
    if few:
        return jnp.where(place < FEW, side * MOST + SLOTS + place, -2)
    if chunk is None:
        return jnp.where(place < MOST, side * MOST + place, -2)
    return FIRST + chunk * CHUNK + side * SLOTS + place


def when_in(bounds_ref, i, chunk, run, otherwise=None):
    first = 0 if chunk is None else FIRST + chunk * CHUNK
    stop = FIRST if chunk is None else first + CHUNK
    here = (bounds_ref[2 * i] < stop) & (bounds_ref[2 * i + 1] > first)
    pl.when(here)(run)
    if otherwise is not None:
        pl.when(jnp.logical_not(here))(otherwise)


def contract(a, b):
    return lax.dot_general(a, b, (((1,), (1,)), ((), ())), preferred_element_type=f32)


def advect_kernel(
    place_ref, spec_ref, land_ref, courant_ref, ways_ref, wind_ref, angle_ref, after_ref,
    used_ref, bounds_ref, slots_ref, speed_ref, high_ref, low_ref, edge_ref, *rest,
):
    sent, (sea_ref, pick_ref, tail_ref) = rest[:-3], rest[-3:]
    group, core = place_ref[0], place_ref[1]
    sea = in_order(land_ref[...]).astype(f32)
    sea_ref[...] = sea

    ramp = [lax.broadcasted_iota(jnp.int32, (COLS, COLS), axis) for axis in (0, 1)]
    upper = jnp.where(ramp[0] <= ramp[1], 1.0, 0.0).astype(bf16)
    running = jnp.dot(sea.astype(bf16), upper, preferred_element_type=f32)
    before = jnp.zeros((1, 1), f32)
    for i in range(ROWS):
        if i == 6:
            before = jnp.maximum(before, 1.0 * FIRST)
        slots_ref[i : i + 1, :] = jnp.where(
            sea[i : i + 1] > 0.0, running[i : i + 1] - 1.0 + before, -1.0
        )
        bounds_ref[2 * i] = jnp.max(before).astype(jnp.int32)
        before = before + running[i : i + 1, COLS - 1 :]
        bounds_ref[2 * i + 1] = jnp.max(before).astype(jnp.int32)
    used_ref[0] = bounds_ref[2 * ROWS - 1]

    frequency, direction = numbered(group * GROUP, HELD)
    speed = look_up(frequency, courant_ref[...])
    across, along = (speed * look_up(direction, ways_ref[i : i + 1, :]) for i in range(2))
    signs = [look_up(direction, ways_ref[i : i + 1, :]) for i in (2, 3)]
    speed_ref[...] = columns([across, along, 1.0 - across - along] + signs, HELD)

    lane = lax.broadcasted_iota(jnp.int32, (1, COLS), 1)
    not_first = jnp.where(lane > 0, 1.0, 0.0)
    not_last = jnp.where(lane < COLS - 1, 1.0, 0.0)

    def advect(first, count, store):
        speeds = [
            jnp.broadcast_to(speed_ref[pl.ds(first, count), i : i + 1], (count, COLS)) for i in range(5)
        ]
        across, along, stay = speeds[:3]
        eastward, northward = (values > 0.5 for values in speeds[3:])

        halves = [jnp.swapaxes(spec_ref[pl.ds(first, count), h], 0, 1) for h in range(COLS // LANES)]

        def row(y):
            i = ORDER.index(y)
            return jnp.concatenate([half[y] for half in halves], axis=1) * sea_ref[i : i + 1, :]

        before, here = jnp.zeros((count, COLS), f32), row(0)
        for y in range(ROWS):
            after = row(y + 1) if y < ROWS - 1 else jnp.zeros((count, COLS), f32)
            west = pltpu.roll(here, 1, 1) * not_first
            east = pltpu.roll(here, COLS - 1, 1) * not_last
            moved = stay * here + across * jnp.where(eastward, west, east)
            moved = moved + along * jnp.where(northward, before, after)
            i = ORDER.index(y)
            store(i, moved * sea_ref[i : i + 1, :])
            before, here = here, after

    def keep(first):
        def store(i, values):
            if i < 6:
                at = slice(i * COLS, (i + 1) * COLS)
                high, low = split(values)
                high_ref[pl.ds(first, TILE), at] = high
                low_ref[pl.ds(first, TILE), at] = low
            else:
                edge_ref[i - 6, pl.ds(first, TILE), :] = values

        return store

    def step(t, carry):
        first = pl.multiple_of(t * TILE, TILE)
        advect(first, TILE, keep(first))
        return carry

    full = GROUP // TILE
    lax.fori_loop(0, full, step, 0)
    last = full * TILE
    left = GROUP - last
    tail_ref[...] = jnp.zeros_like(tail_ref)
    rest_of = slice(last + TILE, HELD)
    for ref in (high_ref, low_ref):
        ref[rest_of, :] = jnp.zeros((HELD - last - TILE, INNER), bf16)
    edge_ref[:, rest_of, :] = jnp.zeros((2, HELD - last - TILE, COLS), f32)

    def keep_tail(i, values):
        tail_ref[i, 0:left, :] = values

    advect(last, left, keep_tail)
    angle = in_order(angle_ref[...])
    for j, values in enumerate((in_order(wind_ref[...]), jnp.cos(angle), jnp.sin(angle))):
        for i in range(ROWS):
            tail_ref[i, left + j : left + j + 1, :] = values[i : i + 1]
    for i in range(ROWS):
        if i < 6:
            at = slice(i * COLS, (i + 1) * COLS)
            high, low = split(tail_ref[i])
            high_ref[last : last + TILE, at] = high
            low_ref[last : last + TILE, at] = low
        else:
            edge_ref[i - 6, last : last + TILE, :] = tail_ref[i]

    def picked(number):
        rows = number.shape[0]
        for i in range(6):
            match(slots_ref, pick_ref.at[:rows, i * COLS : (i + 1) * COLS], number, i)
        pick = pick_ref[:rows, :]
        return contract(high_ref[...], pick) + contract(low_ref[...], pick)

    few = picked(slots_of(core, None, few=True))
    for i, ref in enumerate(sent):
        for half in range(FOLD // BESIDE):
            first = [(half * BESIDE + r) * FOLDED for r in range(BESIDE)]
            runs = [few[n : n + FOLDED, i * LANES : (i + 1) * LANES] for n in first]
            runs = [pltpu.roll(values, r * FEW, 1) if r else values for r, values in enumerate(runs)]
            ref[SENT:, half * LANES : (half + 1) * LANES] = sum(runs)
    line = lax.broadcasted_iota(jnp.int32, (CHUNK, COLS), 0)
    side = jnp.where(line < SLOTS, 0, 1)
    chosen = picked(jnp.bitwise_xor(core, side) * MOST + line - SLOTS * side)
    for i, ref in enumerate(sent):
        ref[:SENT, :] = chosen[:SENT, i * SLOTS : (i + 1) * SLOTS]


def choose(place_ref, bounds_ref, slots_ref, pick_ref, sum_ref, chunk, parts, own_ref, other_ref):
    sum_ref[...] = jnp.zeros_like(sum_ref)
    for i in range(ROWS):

        def add(i=i):
            match(slots_ref, pick_ref, slots_of(place_ref[1], chunk), i)
            high, low = parts(i)
            sum_ref[...] += contract(high, pick_ref[...]) + contract(low, pick_ref[...])

        when_in(bounds_ref, i, chunk, add)
    own_ref[...] = sum_ref[:SENT, :SLOTS]
    other_ref[...] = sum_ref[:SENT, SLOTS:]


def rest_kernel(
    chunks, place_ref, bounds_ref, high_ref, low_ref, edge_ref, south_ref, north_ref, land_ref, slots_ref, speed_ref, *rest
):
    sent, (pick_ref, sum_ref, fixed_ref, edge_high, edge_low) = rest[:-5], rest[-5:]
    core = place_ref[1]
    fixed_ref[...] = edge_ref[...]
    south_row = land_ref[0:1, :].astype(f32)
    north_row = land_ref[ROWS - 1 : ROWS, :].astype(f32)

    def fix(parity):
        for b in range((BLOCKS + 1) // 2):
            at = slice(b * HALF, (b + 1) * HALF)
            north_going, south_going = 2 * b + parity, 2 * b + 1 - parity
            if north_going < BLOCKS:
                mine = slice(north_going * HALF, (north_going + 1) * HALF)
                speed = jnp.broadcast_to(speed_ref[mine, 1:2], (HALF, COLS))
                fixed_ref[0, mine, :] += speed * south_ref[at, :] * south_row
            if south_going < BLOCKS:
                mine = slice(south_going * HALF, (south_going + 1) * HALF)
                speed = jnp.broadcast_to(speed_ref[mine, 1:2], (HALF, COLS))
                fixed_ref[1, mine, :] += speed * north_ref[at, :] * north_row

    for parity in (0, 1):
        pl.when(core == parity)(functools.partial(fix, parity))
    for i in range(2):
        at = slice(i * COLS, (i + 1) * COLS)
        edge_high[:, at], edge_low[:, at] = split(fixed_ref[i])

    def parts(i):
        if i < 6:
            return high_ref[:, i * COLS : (i + 1) * COLS], low_ref[:, i * COLS : (i + 1) * COLS]
        return edge_high[:, (i - 6) * COLS : (i - 5) * COLS], edge_low[:, (i - 6) * COLS : (i - 5) * COLS]

    for n, m in enumerate(chunks):
        choose(place_ref, bounds_ref, slots_ref, pick_ref, sum_ref, m, parts, *sent[2 * n : 2 * n + 2])


def rates_kernel(ways_ref, growth_ref, whitecap_ref, *rate_refs):
    frequency, direction = numbered(0, ALL)
    values = (
        look_up(direction, ways_ref[4:5, :]),
        look_up(direction, ways_ref[5:6, :]),
        substep * look_up(frequency, growth_ref[...]),
        substep * look_up(frequency, whitecap_ref[...]),
    )
    for ref, column in zip(rate_refs, values):
        ref[...] = jnp.broadcast_to(column, (ALL, LANES))


def source_kernel(place_ref, own_ref, pair_ref, far_ref, cross_ref, coupling_ref, *rest):
    rate_refs = rest[:4]
    folded = rest[-1].ndim == 3
    out_ref, back_ref, state_ref, rounded_ref, input_ref, *unfolded = rest[-5 - folded :]
    width = state_ref.shape[1]
    arrived = (own_ref, pair_ref, far_ref, cross_ref)
    group = place_ref[0]

    if folded:
        (flat_ref,) = unfolded
        lane = lax.broadcasted_iota(jnp.int32, (FOLDED, LANES), 1)
        for q, ref in enumerate(arrived):
            for j in range(FOLD):
                half, run = divmod(j, BESIDE)
                moved = ref[SENT:, half * LANES : (half + 1) * LANES]
                moved = pltpu.roll(moved, LANES - run * FEW, 1) if run else moved
                flat_ref[q, j * FOLDED : (j + 1) * FOLDED, :] = jnp.where(lane < FEW, moved, 0.0)

    def load(g):
        for q, ref in enumerate(arrived):
            first = (g ^ q) * GROUP
            state_ref[first : first + GROUP, :SLOTS] = ref[:GROUP, :]
            if folded:
                state_ref[first : first + GROUP, SLOTS:] = flat_ref[q, :GROUP, :]

    for g in range(GROUPS):
        pl.when(group == g)(functools.partial(load, g))
    wind = own_ref[GROUP : GROUP + 3, :]
    if folded:
        wind = jnp.concatenate([wind, flat_ref[0, GROUP : GROUP + 3, :]], axis=1)
    total = set_up(rate_refs, wind, state_ref, rounded_ref.at[0], input_ref)

    def transfer(at):
        return jnp.dot(coupling_ref[at, :], rounded_ref[0], preferred_element_type=f32)

    substeps(group, total, transfer, coupling_ref, rate_refs[3], input_ref, state_ref, rounded_ref, out_ref, back_ref)


def wide(ref, at, width):
    return jnp.concatenate([ref[at, :]] * (width // LANES), axis=1)


def blocks():
    return [slice(start, stop) for start, stop in zip(CUTS[:-1], CUTS[1:])]


def set_up(rate_refs, wind, state_ref, rounded_ref, input_ref):
    width = state_ref.shape[1]
    speed, cosine, sine = (wind[j : j + 1, :] for j in range(3))
    total = jnp.zeros((1, width), f32)
    for at in blocks():
        east, north, growth = (wide(ref, at, width) for ref in rate_refs[:3])
        facing = 0.5 + 0.5 * (east * cosine + north * sine)
        input_ref[at, :] = growth * speed * (facing * facing)
        state = state_ref[at, :]
        rounded_ref[at, :] = state.astype(bf16)
        total = total + jnp.sum(state * state, axis=0, keepdims=True)
    return total


def substeps(group, total, first_transfer, coupling_ref, whitecap_ref, input_ref, state_ref, rounded_ref, out_ref, back_ref):
    width = state_ref.shape[1]

    def update(at, step, damping):
        if step:
            transfer = jnp.dot(coupling_ref[at, :], rounded_ref[step % 2], preferred_element_type=f32)
        else:
            transfer = first_transfer(at)
        state = state_ref[at, :]
        whitecap = wide(whitecap_ref, at, width)
        return state + (substep * transfer + (input_ref[at, :] - whitecap * damping) * state)

    for step in range(SUBSTEPS):
        mean_square = total * (1.0 / ALL)
        damping = mean_square / (1.0 + mean_square)
        total = jnp.zeros((1, width), f32)
        if step < SUBSTEPS - 1:
            for at in blocks():
                values = update(at, step, damping)
                state_ref[at, :] = values
                rounded_ref[(step + 1) % 2, at, :] = values.astype(bf16)
                total = total + jnp.sum(values * values, axis=0, keepdims=True)
        else:
            here = (group // 2) * LOWER
            for start, count in ((0, 464), (464, ALL - LOWER - 464)):
                at = pl.ds(pl.multiple_of(here + start, TILE), count)
                state_ref[at, :] = update(at, step, damping)

    def give(g):
        out_ref[:GROUP, :] = state_ref[g * GROUP : (g + 1) * GROUP, :]
        back_ref[:GROUP, :] = state_ref[(g ^ 1) * GROUP : ((g ^ 1) + 1) * GROUP, :]

    for g in range(GROUPS):
        pl.when(group == g)(functools.partial(give, g))


def ready_kernel(late, place_ref, *rest):
    arrived, coupling_ref, rate_refs = rest[:3], rest[3], rest[4:8]
    state_ref, input_ref, transfer_ref, total_ref, rounded_ref = rest[-5:]
    group = place_ref[0]

    def load(g):
        for q, ref in zip([q for q in range(GROUPS) if q != late], arrived):
            first = (g ^ q) * GROUP
            state_ref[first : first + GROUP, :] = ref[:GROUP, :]
        first = (g ^ late) * GROUP
        state_ref[first : first + GROUP, :] = jnp.zeros((GROUP, SLOTS), f32)

    for g in range(GROUPS):
        pl.when(group == g)(functools.partial(load, g))
    total = set_up(rate_refs, arrived[0][GROUP : GROUP + 3, :], state_ref, rounded_ref, input_ref)
    total_ref[...] = jnp.broadcast_to(total, total_ref.shape)
    for at in blocks():
        transfer_ref[at, :] = jnp.dot(coupling_ref[at, :], rounded_ref[...], preferred_element_type=f32)


def last_kernel(late, place_ref, *rest):
    came_ref, before_ref, input_ref, partial_ref, total_ref, coupling_ref, whitecap_ref = rest[:7]
    out_ref, back_ref, state_ref, rounded_ref, transfer_ref, window_ref = rest[-6:]
    group = place_ref[0]
    came = came_ref[:GROUP, :]
    total = total_ref[0:1, :] + jnp.sum(came * came, axis=0, keepdims=True)
    state_ref[...] = before_ref[...]

    def load(g):
        first = g * GROUP
        start, stop = first // LANES * LANES, min(-(-(first + GROUP) // LANES) * LANES, ALL)
        values = came_ref[:GROUP, :]
        state_ref[first : first + GROUP, :] = values
        window_ref[...] = jnp.zeros_like(window_ref)
        window_ref[first - start : first - start + GROUP, :] = values
        rounded = window_ref[: stop - start, :].astype(bf16)
        for at in blocks():
            transfer_ref[at, :] = partial_ref[at, :] + jnp.dot(
                coupling_ref[at, start:stop], rounded, preferred_element_type=f32
            )

    for g in range(GROUPS):
        pl.when(group == g ^ late)(functools.partial(load, g))
    substeps(
        group, total, lambda at: transfer_ref[at, :], coupling_ref, whitecap_ref, input_ref, state_ref, rounded_ref,
        out_ref, back_ref,
    )


def spread(place_ref, bounds_ref, slots_ref, pick_ref, parts_ref, chunk, sides, values, add, keep=None):
    number = slots_of(place_ref[1], chunk, sides)
    width = number.shape[0]
    for n, ref in enumerate(values):
        at = slice(n * ref.shape[1], (n + 1) * ref.shape[1])
        parts_ref[:SENT, at], parts_ref[SENT:, at] = split(ref[...])

    def grid_row(i, carry):
        def run():
            match(slots_ref, pick_ref.at[:width], number, i)
            both = jnp.dot(parts_ref[:, :width], pick_ref[:width, :], preferred_element_type=f32)
            add(i, both[:SENT] + both[SENT:])

        when_in(bounds_ref, i, chunk, run, keep and functools.partial(keep, i))
        return carry

    lax.fori_loop(0, ROWS, grid_row, 0)


def lanes_of(i):
    return pl.ds(pl.multiple_of(i * COLS, COLS), COLS)


def gather(items, refs, before_ref, sum_ref, pick_ref, parts_ref):
    scalars, slots_ref, values = refs[:2], refs[2], refs[3:]
    for n, (chunk, sides) in enumerate(items):
        own, values = values[: len(sides)], values[len(sides) :]

        def add(i, more, n=n):
            at = lanes_of(i)
            if n:
                sum_ref[:, at] += more
            else:
                sum_ref[:, at] = more if before_ref is None else before_ref[:, at] + more

        def keep(i):
            at = lanes_of(i)
            sum_ref[:, at] = jnp.zeros((SENT, COLS), f32) if before_ref is None else before_ref[:, at]

        spread(*scalars, slots_ref, pick_ref, parts_ref, chunk, sides, own, add, None if n else keep)


def gather_kernel(items, more, *refs):
    refs, (sum_ref, pick_ref, parts_ref) = refs[:-3], refs[-3:]
    refs, before_ref = (refs[:-1], refs[-1]) if more else (refs, None)
    gather(items, refs, before_ref, sum_ref, pick_ref, parts_ref)


def lines_of(i, h):
    y = jnp.where(i < 6, i + 1, jnp.where(i == 6, 0, ROWS - 1))
    return pl.ds(h * ROWS + y, GROUP, stride=LINES)


def finish_kernel(chunk, place_ref, bounds_ref, slots_ref, came_ref, sum_ref, out_ref, pick_ref, parts_ref):
    def keep(i, values=None):
        at = lanes_of(i)
        total = sum_ref[:GROUP, at]
        total = total if values is None else total + values[:GROUP]
        for h in range(COLS // LANES):
            out_ref[lines_of(i, h), :] = total[:, h * LANES : (h + 1) * LANES]

    spread(place_ref, bounds_ref, slots_ref, pick_ref, parts_ref, chunk, (1,), (came_ref,), keep, keep)


def add_kernel(chunk, place_ref, bounds_ref, slots_ref, own_ref, came_ref, sum_ref, out_ref, pick_ref, parts_ref):
    def keep(i, values=None):
        for h in range(COLS // LANES):
            at = lines_of(i, h)
            total = sum_ref[at, :]
            out_ref[at, :] = total if values is None else total + values[:GROUP, h * LANES : (h + 1) * LANES]

    spread(place_ref, bounds_ref, slots_ref, pick_ref, parts_ref, chunk, (0, 1), (own_ref, came_ref), keep, keep)


def call(kernel, out, flops, scratch=(), scalars=1, inputs=0, unread=0, mib=12, moved=8 * MIB, out_scalars=0):
    return pl.pallas_call(
        kernel,
        out_shape=out,
        in_specs=[SCALAR] * scalars + [WHOLE] * inputs + [ANYWHERE] * unread,
        out_specs=(SCALAR,) * out_scalars + (WHOLE,) * (len(out) - out_scalars) if isinstance(out, tuple) else WHOLE,
        scratch_shapes=list(scratch),
        compiler_params=pltpu.CompilerParams(vmem_limit_bytes=mib * MIB),
        cost_estimate=pl.CostEstimate(flops=flops, bytes_accessed=moved, transcendentals=0),
    )


def pairs(flip):
    return [(g, g ^ flip) for g in range(GROUPS)]


def ways():
    bearing = (np.arange(ND) + 0.5) * (2.0 * math.pi / ND)
    cosine, sine = np.cos(bearing), np.sin(bearing)
    rows = [np.abs(cosine), np.abs(sine), cosine > 0, sine > 0, cosine, sine]
    table = np.zeros((ROWS, LANES), np.float32)
    table[: len(rows), :ND] = rows
    return jnp.asarray(table)


def by_lane(values):
    return jnp.pad(values, (0, LANES - NF))[None, :]


def tiled(spectra):
    return spectra.reshape(GROUP, ROWS, COLS // LANES, LANES).swapaxes(1, 2)


def on_device(spectra, land_mask, courant, wind_speed, wind_angle, growth, whitecap, coupling):
    group = lax.axis_index("comp")
    place = jnp.stack([group, group % 2]).astype(jnp.int32)

    halo = jax.ShapeDtypeStruct((PACKED, COLS), f32)
    up, down = call(pack_kernel, (halo, halo), 10**6, inputs=2)(place, tiled(spectra).reshape(GROUP * LINES, LANES), land_mask)
    count = lax.axis_size("pts")
    south = lax.ppermute(up, "pts", [(i, i + 1) for i in range(count - 1)])
    north = lax.ppermute(down, "pts", [(i + 1, i) for i in range(count - 1)])

    message = jax.ShapeDtypeStruct((SENT, SLOTS), f32)
    pick = pltpu.VMEM((CHUNK, COLS), bf16)
    raw = (spectra, land_mask, courant, wind_speed, wind_angle, growth, whitecap)

    def moved_on(raw, after):
        spectra, land_mask, courant, wind_speed, wind_angle, _, _ = raw
        first = jax.ShapeDtypeStruct((SENT_FIRST, SLOTS), f32)
        inner = jax.ShapeDtypeStruct((HELD, INNER), bf16)
        return call(
            advect_kernel,
            (
                jax.ShapeDtypeStruct((1,), jnp.int32),
                jax.ShapeDtypeStruct((2 * ROWS,), jnp.int32),
                jax.ShapeDtypeStruct((ROWS, COLS), f32),
                jax.ShapeDtypeStruct((HELD, LANES), f32),
                inner,
                inner,
                jax.ShapeDtypeStruct((2, HELD, COLS), f32),
                first,
                first,
            ),
            2 * 10**9,
            [
                pltpu.VMEM((ROWS, COLS), f32),
                pltpu.VMEM((CHUNK, INNER), bf16),
                pltpu.VMEM((ROWS, TILE, COLS), f32),
            ],
            inputs=6,
            unread=1,
            mib=16,
            out_scalars=2,
        )(place, tiled(spectra), land_mask, by_lane(courant), ways(), wind_speed, wind_angle, after)

    def rest_of(chunks, moved, land_mask, south, north):
        _, bounds, slots, speeds, high, low, edge, *_ = moved
        return call(
            functools.partial(rest_kernel, chunks),
            (message,) * (2 * len(chunks)),
            4 * 10**9,
            [
                pick,
                pltpu.VMEM((HELD, CHUNK), f32),
                pltpu.VMEM((2, HELD, COLS), f32),
                pltpu.VMEM((HELD, POINTS - INNER), bf16),
                pltpu.VMEM((HELD, POINTS - INNER), bf16),
            ],
            scalars=2,
            inputs=8,
        )(place, bounds, high, low, edge, south, north, land_mask, slots, speeds)

    def rates_of(growth, whitecap):
        return call(rates_kernel, (jax.ShapeDtypeStruct((ALL, LANES), f32),) * 4, 10**6, scalars=0, inputs=3)(
            ways(), by_lane(growth), by_lane(whitecap)
        )

    moved = moved_on(raw, up)
    used, bounds, slots = moved[:3]
    messages = list(moved[7:]) + list(rest_of(range(CHUNKS), moved, land_mask, south, north))
    rates = rates_of(growth, whitecap)

    def worked(coupling, rates, own, other, pair, *after):
        folded = own.shape[0] == SENT_FIRST
        width = WIDE if folded else SLOTS
        far = lax.ppermute(own, "comp", pairs(2))
        cross = lax.ppermute(other, "comp", pairs(3))
        scratch = [pltpu.VMEM((ALL, width), f32), pltpu.VMEM((2, ALL, width), bf16), pltpu.VMEM((ALL, width), f32)]
        out, back = call(
            source_kernel,
            (jax.ShapeDtypeStruct((SENT, width), f32),) * 2,
            4 * 10**9,
            scratch + [pltpu.VMEM((4, HELD, LANES), f32)] * folded,
            inputs=9,
            unread=len(after),
            mib=20 if folded else 18,
        )(place, own, pair, far, cross, coupling, *rates, *after)
        return out, lax.ppermute(back, "comp", pairs(1))

    def worked_late(coupling, rates, own, other, pair, after):
        cross = lax.ppermute(other, "comp", pairs(3))
        far = lax.ppermute(own, "comp", pairs(2))
        whole = jax.ShapeDtypeStruct((ALL, SLOTS), f32)
        late = 2 if LATE_FAR else 3
        last, near = (far, cross) if LATE_FAR else (cross, far)
        made = call(
            functools.partial(ready_kernel, late),
            (whole, whole, whole, jax.ShapeDtypeStruct((ROWS, SLOTS), f32)),
            10**9,
            [pltpu.VMEM((ALL, SLOTS), bf16)],
            inputs=8,
            unread=1,
            mib=20,
        )(place, own, pair, near, coupling, *rates, after)
        window = 5 * LANES
        out, back = call(
            functools.partial(last_kernel, late),
            (message, message),
            10**9,
            [
                pltpu.VMEM((ALL, SLOTS), f32),
                pltpu.VMEM((2, ALL, SLOTS), bf16),
                pltpu.VMEM((ALL, SLOTS), f32),
                pltpu.VMEM((window, SLOTS), f32),
            ],
            inputs=7,
            mib=22,
        )(place, last, *made, coupling, rates[3])
        return out, lax.ppermute(back, "comp", pairs(1))

    def spread_call(kernel, items, out, bounds, slots, values, before=()):
        width = max((WIDE if chunk is None else SLOTS) * len(sides) for chunk, sides in items)
        scratch = [pltpu.VMEM((width, COLS), bf16), pltpu.VMEM((2 * SENT, width), bf16)]
        if kernel is gather_kernel:
            kernel = functools.partial(kernel, items, bool(before))
        else:
            kernel = functools.partial(kernel, items[0][0])
        count = 1 + len(values) + len(before)
        return call(kernel, out, 4 * 10**9, scratch, scalars=2, inputs=count)(
            place, bounds, slots, *values, *before
        )

    sums = jax.ShapeDtypeStruct((SENT, POINTS), f32)
    finished = jax.ShapeDtypeStruct((GROUP * LINES, LANES), f32)
    pair = [lax.ppermute(other, "comp", pairs(1)) for other in messages[1::2]]
    first_out, first_came = worked(coupling, rates, *messages[:2], pair[0], pair[1])
    next_out, next_came = worked(coupling, rates, *messages[2:4], pair[1], first_out, pair[2])
    items = ((None, (0, 1)), (0, (0,)))
    total = spread_call(gather_kernel, items, sums, bounds, slots, (first_out, first_came, next_out))
    last_out, last_came = worked_late(coupling, rates, *messages[4:6], pair[2], total)
    items = ((0, (1,)), (1, (0,)))
    total = spread_call(gather_kernel, items, sums, bounds, slots, (next_came, last_out), (total,))
    result = spread_call(finish_kernel, ((1, (1,)),), finished, bounds, slots, (last_came,), (total,))

    def one_more(result, raw, coupling, south, north):
        moved = moved_on(raw, south)
        own, other = rest_of((CHUNKS,), moved, raw[1], south, north)
        out, came = worked(coupling, rates_of(*raw[-2:]), own, other, lax.ppermute(other, "comp", pairs(1)))
        return spread_call(add_kernel, ((CHUNKS, (0, 1)),), finished, *moved[1:3], (out, came), (result,))

    def no_more(result, *_):
        return result

    result = lax.cond(used[0] > USUAL, one_more, no_more, result, raw, coupling, south, north)
    return result.reshape(GROUP, COLS // LANES, ROWS, LANES).swapaxes(1, 2).reshape(GROUP, ROWS, COLS)


def solution(mesh):
    placed = (
        P("comp", "pts", None),
        P("pts", None),
        P(),
        P("pts", None),
        P("pts", None),
        P(),
        P(),
        P(),
    )
    return jax.shard_map(
        on_device, mesh=mesh, in_specs=placed, out_specs=P("comp", "pts", None), check_vma=False
    )
```
